128 devices in a mesh: seq: 32 (over x, y, core), dp: 4 (over z).
Axes of the slice: x: 4, y: 4, z: 4, core: 2. Of those that a mesh axis runs over, the one named last changes fastest.
Arguments:
- queries: bfloat16 [4, 4096, 2048], P('dp', 'seq'), may hold values from -6 to 6
- keys_in: bfloat16 [4, 4096, 2048], P('dp', 'seq'), may hold values from -9 to 9
- values_in: bfloat16 [4, 4096, 2048], P('dp', 'seq'), may hold values from -6 to 6
- inputs: bfloat16 [4, 4096, 2048], P('dp', 'seq'), may hold values from -6 to 6
- target: bfloat16 [4, 4096, 2048], P('dp', 'seq'), may hold values from -4 to 4
- gate_weight: bfloat16 [2048, 16], replicated, may hold values from -0.125 to 0.125
- beta_bias: float32 [16], replicated, may hold values from -9 to 1.5
Outputs:
- output: bfloat16 [4, 4096, 2048], P('dp', 'seq')
- grad_queries: bfloat16 [4, 4096, 2048], P('dp', 'seq')
- grad_keys: bfloat16 [4, 4096, 2048], P('dp', 'seq')
- grad_values: bfloat16 [4, 4096, 2048], P('dp', 'seq')
- grad_weight: float32 [2048, 16], replicated
The draws below stay inside these ranges and needn't reach their ends.
All inputs are finite; a program needn't handle non-finite values.
Results may differ from the reference program's by a relative error of at most 0.0035.
Values sent between devices are 32-bit elements; how exact they have to be, the bound alone decides.
A program may use at most 256 MiB of HBM per device.

```python
import math
import jax
import jax.numpy as jnp
from jax import lax

HEADS = 16
DK = 128
D = 2048
BLOCK = 128
SEQLEN = 4096
SEQS = 4


def draw_beta_bias(key, part):
    key = jax.random.fold_in(key, 5)
    ranking = jax.random.permutation(jax.random.fold_in(key, 11), HEADS)
    spread = jax.random.uniform(jax.random.fold_in(key, 12), (HEADS,), jnp.float32)
    fast_rate = 0.2 + 0.2 * spread
    slow_rate = DK * 0.6 * jnp.exp(spread * math.log(5.0)) / SEQLEN
    slow_heads = ranking < HEADS // 2
    slow_rate = jnp.minimum(slow_rate, 0.4)
    decay_rate = jnp.where(slow_heads, slow_rate, fast_rate).astype(jnp.float32)
    return jnp.log(2.0 * decay_rate) - jnp.log(1.0 - 2.0 * decay_rate)


def draw_keys_in(key, part):
    key = jax.random.fold_in(key, 21)
    shared = jnp.clip(jax.random.normal(jax.random.fold_in(key, 1), (SEQS, 1, D), jnp.float32), -3.0, 3.0)
    noise = jnp.clip(jax.random.normal(jax.random.fold_in(key, 2), (SEQS, SEQLEN, D), jnp.float32), -4.0, 4.0)
    amplitude = 1.5
    return (amplitude * shared + noise).astype(jnp.bfloat16)


def block_scale(own_key, dims, cuts, smallest, high):
    def one(axis_at, shards_of):
        heights = jax.random.uniform(jax.random.fold_in(jax.random.fold_in(own_key, 6), axis_at), (shards_of,), jnp.float32, smallest / len(cuts), high / len(cuts))
        return jnp.repeat(jnp.exp(heights), dims[axis_at] // shards_of).reshape((-1,) + (1,) * (len(dims) - axis_at - 1))

    factor_of = one(*cuts[0])
    for cut in cuts[1:]:
        factor_of = factor_of * one(*cut)
    return factor_of


def centred(key, dims, scale, limit, cuts=(), kind=jnp.bfloat16):
    loudness = block_scale(key, dims, cuts, -0.22, 0.18) if cuts else 1.0
    drawn = jax.random.normal(key, dims, jnp.float32) * scale * loudness
    return jnp.minimum(jnp.maximum(drawn, -limit), limit).astype(kind)


def setup_inputs(seed: int = 0) -> dict:
    key_list = jax.random.split(jax.random.key(seed), 8)
    queries = centred(key_list[0], (SEQS, SEQLEN, D), 1.0, 6.0, ((0, 4), (1, 32)))
    keys_in = draw_keys_in(jax.random.fold_in(key_list[7], 71), 0)
    values_in = centred(key_list[2], (SEQS, SEQLEN, D), 1.0, 6.0, ((0, 4), (1, 32)))
    inputs = centred(key_list[3], (SEQS, SEQLEN, D), 1.0, 6.0, ((0, 4), (1, 32)))
    target = centred(key_list[4], (SEQS, SEQLEN, D), 0.5, 4.0, ((0, 4), (1, 32)))
    gate_weight = centred(key_list[5], (D, HEADS), D ** -0.5, 0.125)
    beta_bias = draw_beta_bias(jax.random.fold_in(key_list[7], 71), 0)
    return dict(queries=queries, keys_in=keys_in, values_in=values_in, inputs=inputs, target=target, gate_weight=gate_weight, beta_bias=beta_bias)


epsilon = 1e-06
highest_precision = lax.Precision.HIGHEST

def unit_rows(matrix):
    return matrix * lax.rsqrt(lax.optimization_barrier(jnp.sum(matrix * matrix, axis=-1, keepdims=True)) + epsilon)

def block_terms(queries, keys_in, values_in, logits):
    length = queries.shape[0]
    head_count = logits.shape[1]
    head_width = queries.shape[1] // head_count
    blocks = length // BLOCK

    def arrange(matrix):
        return matrix.reshape(blocks, BLOCK, head_count, head_width).transpose(0, 2, 1, 3)
    query_unit = unit_rows(arrange(queries.astype(jnp.float32)))
    key_unit = unit_rows(arrange(keys_in.astype(jnp.float32)))
    value_rows = arrange(values_in.astype(jnp.float32))
    strength = (0.5 * jax.nn.sigmoid(logits)).reshape(blocks, BLOCK, head_count).transpose(0, 2, 1)[..., None]
    key_gram = jnp.einsum('nhik,nhjk->nhij', key_unit, key_unit, precision=highest_precision)
    lower_mask = jnp.tril(jnp.ones((BLOCK, BLOCK), jnp.float32), -1)
    system = jnp.eye(BLOCK, dtype=jnp.float32) + lower_mask * strength * key_gram
    right_side = jnp.concatenate([strength * key_unit, strength * value_rows], axis=-1)
    solved = jax.scipy.linalg.solve_triangular(system, right_side, lower=True)
    write_keys = solved[..., :head_width]
    write_values = solved[..., head_width:]
    inclusive = jnp.tril(jnp.ones((BLOCK, BLOCK), jnp.float32))
    scores = inclusive * jnp.einsum('nhik,nhjk->nhij', query_unit, key_unit, precision=highest_precision)
    return (query_unit, key_unit, write_keys, write_values, scores)

def state_pass(terms, entry_state):

    def advance(carried_state, block_parts):
        block_queries, block_keys, write_keys, write_values, score_block = block_parts
        delta_correction = write_values - jnp.einsum('fbi,fir->fbr', write_keys, carried_state, precision=highest_precision)
        produced_output = jnp.einsum('fbi,fir->fbr', block_queries, carried_state, precision=highest_precision)
        produced_output = produced_output + jnp.einsum('hcj,hjv->hcv', score_block, delta_correction, precision=highest_precision)
        carried_state = carried_state + jnp.einsum('nrm,nrp->nmp', block_keys, delta_correction, precision=highest_precision)
        return (carried_state, produced_output)
    final_state, produced_output = lax.scan(advance, entry_state, terms)
    blocks, head_count, rows_block, head_width = produced_output.shape
    flat = produced_output.transpose(0, 2, 1, 3).reshape(blocks * rows_block, head_count * head_width)
    return (flat, final_state)

def one_sequence(queries, keys_in, values_in, inputs, target, gate_weight, beta_bias):
    head_count = gate_weight.shape[1]
    head_width = queries.shape[1] // head_count
    logits = jnp.dot(inputs.astype(jnp.float32), gate_weight.astype(jnp.float32), preferred_element_type=jnp.float32) + beta_bias

    def forward(queries, keys_in, values_in, logits):
        terms = block_terms(queries, keys_in, values_in, logits)
        entry_state = jnp.zeros((head_count, head_width, head_width), jnp.float32)
        return state_pass(terms, entry_state)[0]
    produced_output, pullback = jax.vjp(forward, queries, keys_in, values_in, logits)
    rounded = lax.optimization_barrier(produced_output.astype(jnp.bfloat16))
    cotangent = rounded.astype(jnp.float32) - target.astype(jnp.float32)
    grad_q, grad_k, grad_v, grad_logits = pullback(cotangent)
    grad_gate = jnp.dot(inputs.T.astype(jnp.float32), grad_logits.astype(jnp.float32), preferred_element_type=jnp.float32, precision=highest_precision)
    return (rounded, grad_q, grad_k, grad_v, grad_gate)

def reference(queries, keys_in, values_in, inputs, target, gate_weight, beta_bias):

    def single(sequence_parts):
        return one_sequence(*sequence_parts, gate_weight, beta_bias)
    rounded, grad_q, grad_k, grad_v, grad_gate = lax.map(single, (queries, keys_in, values_in, inputs, target))
    scaled = lax.optimization_barrier(jnp.sum(grad_gate, axis=0)) * (1.0 / math.sqrt(SEQS * SEQLEN))
    return (rounded, grad_q, grad_k, grad_v, scaled)
```

```python
import functools
import math

import jax
import jax.numpy as jnp
from jax import lax
from jax.experimental import pallas as pl
from jax.experimental.pallas import tpu as pltpu
from jax.sharding import PartitionSpec as P

BLOCK = 128
EPSILON = 1e-06
GROUP = 4
f32 = jnp.float32
bf16 = jnp.bfloat16
MESH = pl.DeviceIdType.MESH


def mm(a, b):
    return jnp.dot(a, b, preferred_element_type=f32)


def mm_rows(a, b):
    return lax.dot_general(a, b, (((1,), (1,)), ((), ())), preferred_element_type=f32)


def mm3(a, b):
    return jnp.dot(a, b, preferred_element_type=f32, precision=lax.Precision.HIGH)


def split(x):
    high = x.astype(bf16)
    return high, (x - high.astype(f32)).astype(bf16)


def left_exact(exact, x):
    high, low = split(x)
    return mm(exact, high) + mm(exact, low)


def right_exact(x, exact):
    high, low = split(x)
    return mm(high, exact) + mm(low, exact)


def masks():
    row = lax.broadcasted_iota(jnp.int32, (BLOCK, BLOCK), 0)
    col = lax.broadcasted_iota(jnp.int32, (BLOCK, BLOCK), 1)
    return row, col


def unit_lower_inverse(systems):
    row, col = masks()
    apart = row ^ col
    eye = (row == col).astype(f32)
    inverses = [eye - jnp.where(apart < 2, a, 0.0) for a in systems]
    size = 2
    while size < BLOCK:
        band = (apart >= size) & (apart < 2 * size)
        packed = [x.astype(bf16) for x in inverses]
        steps = [mm(jnp.where(band, a, 0.0).astype(bf16), x) for a, x in zip(systems, packed)]
        steps = [mm(x, y.astype(bf16)) for x, y in zip(packed, steps)]
        inverses = [x - y for x, y in zip(inverses, steps)]
        size *= 2
    rest = [mm3(a, x) for a, x in zip(systems, inverses)]
    rest = [(eye - x - y) for x, y in zip(inverses, rest)]
    fixes = [mm(x.astype(bf16), y.astype(bf16)) for x, y in zip(inverses, rest)]
    return [x + y for x, y in zip(inverses, fixes)]


def kernel(
    chips,
    q_ref, k_ref, v_ref, x_ref, t_ref, w_ref, b_ref,
    o_ref, gq_ref, gk_ref, gv_ref, gw_ref,
    strength, rk_col, rq_col, be_col, rk_row,
    key_t, query_t, gram_s, inv_s, inv_t, wk_s, wv_s, p_s, p_t, z_s,
    f_s, f_t, s_t, do_s, e_s, dpq_s, dl_s,
    maps, out_map, chip_map, got_map, prefix, state_out, hand_in, state_in, s_own, s_sib, s_out,
    c_both, c_out, c_chip, c_got, suffix, map_t, grad_out, gh_in, grad_in, g_own, g_sib, g_out,
    send, recv,
):
    me = lax.axis_index("seq")
    core = lax.rem(me, 2)
    chip = lax.div(me, 2)
    half = chips // 2
    part = lax.div(chip, half)
    place = lax.rem(chip, half)
    parity = lax.rem(chip, 2)
    sibling = me + 1 - 2 * core
    rounds = half // min(GROUP, half)
    group = min(GROUP, half)

    def owner(j):
        return 2 * (2 * j + core) + part

    def source(i):
        return 2 * (half * core + i) + parity

    def push(kind, at, src, dst, target):
        return pltpu.make_async_remote_copy(
            src_ref=src, dst_ref=dst, send_sem=send.at[kind, at], recv_sem=recv.at[kind, at],
            device_id={"seq": target}, device_id_type=MESH,
        )

    def wait_in(kind, at, dst):
        push(kind, at, dst, dst, sibling).wait_recv()

    def route(kind, send_at, recv_at, src, dst, target):
        @pl.when(target != me)
        def _():
            pltpu.make_async_remote_copy(
                src_ref=src, dst_ref=dst, send_sem=send.at[kind, send_at], recv_sem=recv.at[kind, recv_at],
                device_id={"seq": target}, device_id_type=MESH,
            ).start()

        @pl.when(target == me)
        def _():
            dst[...] = src[...]

    def routed(kind, at, dst, origin):
        @pl.when(origin != me)
        def _():
            wait_in(kind, at, dst)

    barrier = pltpu.get_barrier_semaphore()

    def greet(target):
        @pl.when(target != me)
        def _():
            pl.semaphore_signal(barrier, inc=1, device_id={"seq": target}, device_id_type=MESH)

    pl.semaphore_signal(barrier, inc=1, device_id={"seq": sibling}, device_id_type=MESH)
    for j in range(half):
        greet(owner(j))
        greet(source(j))

    logits = mm(x_ref[...], w_ref[...]) + b_ref[...]
    strength[...] = 0.5 / (1.0 + jnp.exp(-logits))
    dl_s[...] = jnp.zeros_like(dl_s)

    own_self = (part == core) & (parity == core)

    @pl.when(own_self)
    def _():
        pl.semaphore_wait(barrier, 2 * half - 1)

    @pl.when(jnp.logical_not(own_self))
    def _():
        pl.semaphore_wait(barrier, 2 * half + 1)

    def span(head):
        return pl.ds(pl.multiple_of(head * BLOCK, BLOCK), BLOCK)

    def own_head(j):
        return 2 * j + core

    def other_head(j):
        return 2 * j + 1 - core

    def local_maps(slots, heads):
        row, col = masks()
        eye = row == col
        keys = [k_ref[:, span(h)] for h in heads]
        values = [v_ref[:, span(h)] for h in heads]
        strengths = strength[...]
        lane = lax.broadcasted_iota(jnp.int32, strengths.shape, 1)
        products = [mm_rows(key, key) for key in keys]
        norms = [jnp.where(eye, product, 0.0) for product in products]
        rks = [lax.rsqrt(jnp.sum(n, axis=1, keepdims=True) + EPSILON) for n in norms]
        rkr = [lax.rsqrt(jnp.sum(n, axis=0, keepdims=True) + EPSILON) for n in norms]
        bes = [jnp.sum(jnp.where(lane == h, strengths, 0.0), axis=1, keepdims=True) for h in heads]
        ber = [jnp.sum(jnp.where(eye, be, 0.0), axis=0, keepdims=True) for be in bes]
        grams = [jnp.where(row > col, m * a * b, 0.0) for m, a, b in zip(products, rks, rkr)]
        inverses = unit_lower_inverse([g * be for g, be in zip(grams, bes)])
        weights = [x * b for x, b in zip(inverses, ber)]
        wks = [right_exact(w * r, key) for w, r, key in zip(weights, rkr, keys)]
        wvs = [right_exact(w, value) for w, value in zip(weights, values)]
        keys_t = [key.T for key in keys]
        both = [
            left_exact(kt, jnp.concatenate([a, b], axis=1) * r) for kt, a, b, r in zip(keys_t, wks, wvs, rks)
        ]
        for i, s in enumerate(slots):
            rk_col[s] = rks[i]
            be_col[s] = bes[i]
            rk_row[s] = rkr[i]
            gram_s[s] = grams[i]
            inv_s[s] = inverses[i]
            wk_s[s] = wks[i]
            wv_s[s] = wvs[i]
            key_t[s] = keys_t[i]
        eyef = eye.astype(f32)
        return [jnp.concatenate([eyef - m[:, :BLOCK], m[:, BLOCK:]], axis=1) for m in both]

    def steps(body):
        def run(r, carry):
            body([r * group + u for u in range(group)])
            return carry

        lax.fori_loop(0, rounds, run, 0)

    def first_other(js):
        made = local_maps([half + j for j in js], [other_head(j) for j in js])
        for j, m in zip(js, made):
            out_map[j] = m
        for j in js:
            push(0, j, out_map.at[j], maps.at[core, j], sibling).start()

    steps(first_other)

    def first_own(js):
        made = local_maps(js, [own_head(j) for j in js])
        for j, m in zip(js, made):
            maps[core, j] = m
        for j in js:
            wait_in(0, j, maps.at[1 - core, j])
        zero = jnp.zeros((BLOCK, BLOCK), f32)
        earlier = [maps[0, j] for j in js]
        later = [maps[1, j] for j in js]
        made = [mm3(b[:, :BLOCK], a) for a, b in zip(earlier, later)]
        for j, m, b in zip(js, made, later):
            chip_map[j] = m + jnp.concatenate([zero, b[:, BLOCK:]], axis=1)
        for j in js:
            route(1, j, place, chip_map.at[j], got_map.at[place], owner(j))

    steps(first_own)

    def score_terms(slots, heads):
        row, col = masks()
        keys = [k_ref[:, span(h)] for h in heads]
        queries = [q_ref[:, span(h)] for h in heads]
        rkr = [rk_row[s] for s in slots]
        products = [mm_rows(q, k) for q, k in zip(queries, keys)]
        wide = [q.astype(f32) for q in queries]
        rqs = [lax.rsqrt(jnp.sum(q * q, axis=1, keepdims=True) + EPSILON) for q in wide]
        ps = [jnp.where(row >= col, m * a * b, 0.0) for m, a, b in zip(products, rqs, rkr)]
        inverses_t = [inv_s[s].T for s in slots]
        zs = [right_exact(x * r, k) for x, r, k in zip(inverses_t, rkr, keys)]
        for i, s in enumerate(slots):
            rq_col[s] = rqs[i]
            p_s[s] = ps[i]
            p_t[s] = ps[i].T
            inv_t[s] = inverses_t[i]
            z_s[s] = zs[i]
            query_t[s] = queries[i].T

    steps(lambda js: score_terms(js, [own_head(j) for j in js]))
    steps(lambda js: score_terms([half + j for j in js], [other_head(j) for j in js]))

    row, col = masks()
    eyef = (row == col).astype(f32)
    zero = jnp.zeros((BLOCK, BLOCK), f32)

    slot = lax.div(chip, 2)

    @pl.when(core == 0)
    def _():
        state_out[0] = zero

        def lap(i, carry):
            routed(1, i, got_map.at[i], source(i))
            route(3, i, slot, state_out.at[i], state_in.at[slot], source(i))
            step = got_map[i]
            state_out[i + 1] = mm3(step[:, :BLOCK], state_out[i]) + step[:, BLOCK:]
            return carry

        lax.fori_loop(0, half, lap, 0)
        push(2, 0, state_out.at[half], hand_in.at[0], sibling).start()
        suffix[half] = eyef

        def back(n, carry):
            i = half - 1 - n
            turned = got_map[i][:, :BLOCK].T
            map_t[i] = turned
            suffix[i] = mm3(turned, suffix[i + 1])
            return carry

        lax.fori_loop(0, half, back, 0)

    @pl.when(core == 1)
    def _():
        prefix[0] = jnp.concatenate([eyef, zero], axis=1)

        def lap(i, carry):
            routed(1, i, got_map.at[i], source(i))
            step = got_map[i]
            map_t[i] = step[:, :BLOCK].T
            prefix[i + 1] = mm3(step[:, :BLOCK], prefix[i]) + jnp.concatenate([zero, step[:, BLOCK:]], axis=1)
            return carry

        lax.fori_loop(0, half, lap, 0)
        wait_in(2, 0, hand_in.at[0])
        entry = hand_in[0]

        def lift(r, carry):
            for u in range(group):
                i = r * group + u
                known = prefix[i]
                state_out[i] = mm3(known[:, :BLOCK], entry) + known[:, BLOCK:]
            for u in range(group):
                i = r * group + u
                route(3, i, slot, state_out.at[i], state_in.at[slot], source(i))
            return carry

        lax.fori_loop(0, rounds, lift, 0)

    def enter(j, carry):
        routed(3, j, state_in.at[j], owner(j))
        first = state_in[j]
        step = maps[0, j]
        second = mm3(step[:, :BLOCK], first) + step[:, BLOCK:]
        s_own[j] = jnp.where(core == 0, first, second)
        s_out[j] = jnp.where(core == 0, second, first)
        push(4, j, s_out.at[j], s_sib.at[j], sibling).start()
        return carry

    lax.fori_loop(0, half, enter, 0)

    def forward(slots, heads, states):
        queries = [q_ref[:, span(h)] for h in heads]
        rqs = [rq_col[s] for s in slots]
        fresh = [wv_s[s] - mm3(wk_s[s], state) for s, state in zip(slots, states)]
        read = [left_exact(q, state) * r for q, state, r in zip(queries, states, rqs)]
        outs = [o + mm3(p_s[s], f) for o, f, s in zip(read, fresh, slots)]
        outs = [o.astype(bf16) for o in outs]
        cots = [o.astype(f32) - t_ref[:, span(h)].astype(f32) for o, h in zip(outs, heads)]
        ups = [mm3(p_t[s], d) for d, s in zip(cots, slots)]
        es = [mm3(inv_t[s], u) for u, s in zip(ups, slots)]
        cs = [left_exact(query_t[s], d * r) for s, d, r in zip(slots, cots, rqs)]
        cs = [c - left_exact(key_t[s], e * (rk_col[s] * be_col[s])) for c, s, e in zip(cs, slots, es)]
        for i, (s, h) in enumerate(zip(slots, heads)):
            o_ref[:, span(h)] = outs[i]
            f_s[s] = fresh[i]
            do_s[s] = cots[i]
            e_s[s] = es[i]
        return cs

    def second_own(js):
        made = forward(js, [own_head(j) for j in js], [s_own[j] for j in js])
        for j, c in zip(js, made):
            c_both[core, j] = c

    steps(second_own)

    def second_other(js):
        for j in js:
            wait_in(4, j, s_sib.at[j])
        made = forward([half + j for j in js], [other_head(j) for j in js], [s_sib[j] for j in js])
        for j, c in zip(js, made):
            c_out[j] = c
        for j in js:
            push(5, j, c_out.at[j], c_both.at[core, j], sibling).start()

    steps(second_other)

    def join_grads(js):
        for j in js:
            wait_in(5, j, c_both.at[1 - core, j])
        made = [mm3(maps[0, j][:, :BLOCK].T, c_both[1, j]) + c_both[0, j] for j in js]
        for j, c in zip(js, made):
            c_chip[j] = c
        for j in js:
            route(6, j, place, c_chip.at[j], c_got.at[place], owner(j))

    steps(join_grads)

    def query_grads(slots, heads, states):
        row, col = masks()
        fts = [f_s[s].T for s in slots]
        sts = [state.T for state in states]
        cots = [do_s[s] for s in slots]
        rqs = [rq_col[s] for s in slots]
        dps = [jnp.where(row >= col, mm3(d, ft), 0.0) for d, ft in zip(cots, fts)]
        dqs = [mm3(d, st) for d, st in zip(cots, sts)]
        dqs = [
            d + right_exact(p * rk_row[s], k_ref[:, span(h)]) for d, p, s, h in zip(dqs, dps, slots, heads)
        ]
        turned = [right_exact((p * r).T, q_ref[:, span(h)]) for p, r, h in zip(dps, rqs, heads)]
        for i, (s, h) in enumerate(zip(slots, heads)):
            unit = q_ref[:, span(h)].astype(f32) * rqs[i]
            grad = rqs[i] * (dqs[i] - unit * jnp.sum(unit * dqs[i], axis=1, keepdims=True))
            gq_ref[:, span(h)] = grad.astype(bf16)
            dpq_s[s] = turned[i]
            f_t[s] = fts[i]
            s_t[s] = sts[i]

    steps(lambda js: query_grads(js, [own_head(j) for j in js], [s_own[j] for j in js]))
    steps(
        lambda js: query_grads(
            [half + j for j in js], [other_head(j) for j in js], [s_sib[j] for j in js]
        )
    )

    grad_out[half] = zero

    @pl.when(core == 1)
    def _():
        def lap(n, carry):
            i = half - 1 - n
            routed(6, i, c_got.at[i], source(i))
            route(8, i, slot, grad_out.at[i + 1], grad_in.at[slot], source(i))
            grad_out[i] = mm3(map_t[i], grad_out[i + 1]) + c_got[i]
            return carry

        lax.fori_loop(0, half, lap, 0)
        push(7, 0, grad_out.at[0], gh_in.at[0], sibling).start()

    @pl.when(core == 0)
    def _():
        def lap(n, carry):
            i = half - 1 - n
            routed(6, i, c_got.at[i], source(i))
            grad_out[i] = mm3(map_t[i], grad_out[i + 1]) + c_got[i]
            return carry

        lax.fori_loop(0, half, lap, 0)
        wait_in(7, 0, gh_in.at[0])
        entry = gh_in[0]

        def lift(r, carry):
            for u in range(group):
                i = half - 1 - (r * group + u)
                grad_out[i + 1] = mm3(suffix[i + 1], entry) + grad_out[i + 1]
            for u in range(group):
                i = half - 1 - (r * group + u)
                route(8, i, slot, grad_out.at[i + 1], grad_in.at[slot], source(i))
            return carry

        lax.fori_loop(0, rounds, lift, 0)

    def leave(j, carry):
        routed(8, j, grad_in.at[j], owner(j))
        last = grad_in[j]
        inner = mm3(maps[1, j][:, :BLOCK].T, last) + c_both[1, j]
        g_own[j] = jnp.where(core == 0, inner, last)
        g_out[j] = jnp.where(core == 0, last, inner)
        push(9, j, g_out.at[j], g_sib.at[j], sibling).start()
        return carry

    lax.fori_loop(0, half, leave, 0)

    def backward(slots, heads, grads):
        row, col = masks()
        es = [e_s[s] + mm3(z_s[s], g) for s, g in zip(slots, grads)]
        gts = [g.T for g in grads]
        efs = [jnp.where(row > col, mm3(e, f_t[s]), 0.0) for e, s in zip(es, slots)]
        ess = [mm3(e, s_t[s]) for e, s in zip(es, slots)]
        dks = [dpq_s[s] + mm3(f_s[s], gt) for s, gt in zip(slots, gts)]
        bes = [be_col[s] for s in slots]
        links = [ef * be for ef, be in zip(efs, bes)]
        links = [(m + m.T) * rk_row[s] for m, s in zip(links, slots)]
        dks = [d - es_ * be for d, es_, be in zip(dks, ess, bes)]
        dks = [d - right_exact(m, k_ref[:, span(h)]) for d, m, h in zip(dks, links, heads)]
        added = 0.0
        lane = lax.broadcasted_iota(jnp.int32, (BLOCK, BLOCK), 1)
        for i, (s, h) in enumerate(zip(slots, heads)):
            rk = rk_col[s]
            unit = k_ref[:, span(h)].astype(f32) * rk
            grad = rk * (dks[i] - unit * jnp.sum(unit * dks[i], axis=1, keepdims=True))
            gk_ref[:, span(h)] = grad.astype(bf16)
            gv_ref[:, span(h)] = (es[i] * bes[i]).astype(bf16)
            terms = es[i] * v_ref[:, span(h)].astype(f32) - ess[i] * unit - efs[i] * gram_s[s]
            dl = jnp.sum(terms, axis=1, keepdims=True) * (bes[i] * (1.0 - 2.0 * bes[i]))
            added = added + jnp.where(lane == h, dl, 0.0)
        dl_s[...] += added

    steps(lambda js: backward(js, [own_head(j) for j in js], [g_own[j] for j in js]))

    def last_other(js):
        for j in js:
            wait_in(9, j, g_sib.at[j])
        backward([half + j for j in js], [other_head(j) for j in js], [g_sib[j] for j in js])

    steps(last_other)

    heads = 2 * half
    gate = dl_s[...].T
    high, low = split(gate[:heads])
    gw_ref[...] = mm(high, x_ref[...]) + mm(low, x_ref[...])

    def drain(j, carry):
        push(0, j, out_map.at[j], out_map.at[j], sibling).wait_send()
        push(4, j, s_out.at[j], s_out.at[j], sibling).wait_send()
        push(5, j, c_out.at[j], c_out.at[j], sibling).wait_send()
        push(9, j, g_out.at[j], g_out.at[j], sibling).wait_send()

        @pl.when(owner(j) != me)
        def _():
            push(1, j, chip_map.at[j], chip_map.at[j], sibling).wait_send()
            push(6, j, c_chip.at[j], c_chip.at[j], sibling).wait_send()

        @pl.when(source(j) != me)
        def _():
            push(3, j, state_out.at[j], state_out.at[j], sibling).wait_send()
            push(8, j, grad_out.at[j + 1], grad_out.at[j + 1], sibling).wait_send()

        return carry

    lax.fori_loop(0, half, drain, 0)

    @pl.when(core == 0)
    def _():
        push(2, 0, state_out.at[half], state_out.at[half], sibling).wait_send()

    @pl.when(core == 1)
    def _():
        push(7, 0, grad_out.at[0], grad_out.at[0], sibling).wait_send()


def shards(chips, queries, keys_in, values_in, inputs, target, gate_weight, beta_bias):
    heads = gate_weight.shape[1]
    width = heads * BLOCK
    half = heads // 2
    square = (BLOCK, BLOCK)

    def many(count, *tail, kind=f32):
        return pltpu.VMEM((count,) + (tail or square), kind)

    wide = (BLOCK, 2 * BLOCK)
    scratch = [
        pltpu.VMEM((BLOCK, heads), f32), many(heads, BLOCK, 1), many(heads, BLOCK, 1), many(heads, BLOCK, 1),
        many(heads, 1, BLOCK),
        many(heads, kind=bf16), many(heads, kind=bf16),
    ] + [many(heads)] * 8 + [many(heads)] * 6 + [
        pltpu.VMEM(square, f32),
        pltpu.VMEM((2, half) + wide, f32), many(half, *wide), many(half, *wide), many(half, *wide),
        many(half + 1, *wide), many(half + 1), many(1), many(half), many(half), many(half), many(half),
        pltpu.VMEM((2, half) + square, f32), many(half), many(half), many(half), many(half + 1), many(half),
        many(half + 1), many(1), many(half), many(half), many(half), many(half),
        pltpu.SemaphoreType.DMA((10, half)), pltpu.SemaphoreType.DMA((10, half)),
    ]
    rows = jax.ShapeDtypeStruct((BLOCK, width), bf16)
    whole = pl.BlockSpec(memory_space=pltpu.VMEM)
    results = pl.pallas_call(
        functools.partial(kernel, chips),
        out_shape=(rows, rows, rows, rows, jax.ShapeDtypeStruct((heads, inputs.shape[-1]), f32)),
        in_specs=[whole] * 7,
        out_specs=(whole,) * 5,
        scratch_shapes=scratch,
        compiler_params=pltpu.CompilerParams(
            collective_id=0, has_side_effects=True, vmem_limit_bytes=52 * 1024 * 1024
        ),
    )(queries[0], keys_in[0], values_in[0], inputs[0], target[0], gate_weight, beta_bias[None])
    output, grad_q, grad_k, grad_v, local_weight = results
    total = lax.psum(local_weight, ("seq", "dp"))
    tokens = BLOCK * lax.axis_size("seq") * lax.axis_size("dp")
    scaled = total.T * (1.0 / math.sqrt(tokens))
    return (output[None], grad_q[None], grad_k[None], grad_v[None], scaled)


def solution(mesh):
    placed = P("dp", "seq", None)
    chips = mesh.shape["seq"] // 2
    return jax.shard_map(
        functools.partial(shards, chips),
        mesh=mesh,
        in_specs=(placed,) * 5 + (P(), P()),
        out_specs=(placed,) * 4 + (P(),),
        check_vma=False,
    )
```

```python
import functools
import math

import jax
import jax.numpy as jnp
from jax import lax
from jax.experimental import pallas as pl
from jax.experimental.pallas import tpu as pltpu
from jax.sharding import PartitionSpec as P

BLOCK = 128
EPSILON = 1e-06
GROUP = 4
f32 = jnp.float32
bf16 = jnp.bfloat16
MESH = pl.DeviceIdType.MESH


def mm(a, b):
    return jnp.dot(a, b, preferred_element_type=f32)


def mm_rows(a, b):
    return lax.dot_general(a, b, (((1,), (1,)), ((), ())), preferred_element_type=f32)


def mm3(a, b):
    return jnp.dot(a, b, preferred_element_type=f32, precision=lax.Precision.HIGH)


def split(x):
    high = x.astype(bf16)
    return high, (x - high.astype(f32)).astype(bf16)


def left_exact(exact, x):
    high, low = split(x)
    return mm(exact, high) + mm(exact, low)


def right_exact(x, exact):
    high, low = split(x)
    return mm(high, exact) + mm(low, exact)


def masks():
    row = lax.broadcasted_iota(jnp.int32, (BLOCK, BLOCK), 0)
    col = lax.broadcasted_iota(jnp.int32, (BLOCK, BLOCK), 1)
    return row, col


def unit_lower_inverse(systems):
    row, col = masks()
    apart = row ^ col
    eye = (row == col).astype(f32)
    inverses = [eye - jnp.where(apart < 2, a, 0.0) for a in systems]
    size = 2
    while size < BLOCK:
        band = (apart >= size) & (apart < 2 * size)
        packed = [x.astype(bf16) for x in inverses]
        steps = [mm(jnp.where(band, a, 0.0).astype(bf16), x) for a, x in zip(systems, packed)]
        steps = [mm(x, y.astype(bf16)) for x, y in zip(packed, steps)]
        inverses = [x - y for x, y in zip(inverses, steps)]
        size *= 2
    rest = [mm3(a, x) for a, x in zip(systems, inverses)]
    rest = [(eye - x - y) for x, y in zip(inverses, rest)]
    fixes = [mm(x.astype(bf16), y.astype(bf16)) for x, y in zip(inverses, rest)]
    return [x + y for x, y in zip(inverses, fixes)]


def kernel(
    chips, depth, scale,
    q_ref, k_ref, v_ref, x_ref, t_ref, w_ref, b_ref,
    o_ref, gq_ref, gk_ref, gv_ref, gw_ref,
    strength, rk_col, rq_col, be_col, rk_row,
    key_t, query_t, gram_s, inv_s, inv_t, wk_s, wv_s, p_s, p_t, z_s,
    f_s, f_t, s_t, do_s, e_s, dpq_s, dl_s,
    maps, out_map, chip_map, got_map, prefix, state_out, hand_in, state_in, s_own, s_sib, s_out,
    c_both, c_out, c_chip, c_got, suffix, map_t, grad_out, gh_in, grad_in, g_own, g_sib, g_out,
    gate_own, gate_other, gate_in, depth_out, depth_in, tile_out, tiles,
    send, recv, gate_send, gate_recv, depth_send, depth_recv,
):
    me = lax.axis_index("seq")
    core = lax.rem(me, 2)
    chip = lax.div(me, 2)
    half = chips // 2
    part = lax.div(chip, half)
    place = lax.rem(chip, half)
    parity = lax.rem(chip, 2)
    sibling = me + 1 - 2 * core
    rounds = half // min(GROUP, half)
    group = min(GROUP, half)

    def owner(j):
        return 2 * (2 * j + core) + part

    def source(i):
        return 2 * (half * core + i) + parity

    def push(kind, at, src, dst, target):
        return pltpu.make_async_remote_copy(
            src_ref=src, dst_ref=dst, send_sem=send.at[kind, at], recv_sem=recv.at[kind, at],
            device_id={"seq": target}, device_id_type=MESH,
        )

    def wait_in(kind, at, dst):
        push(kind, at, dst, dst, sibling).wait_recv()

    def route(kind, send_at, recv_at, src, dst, target):
        @pl.when(target != me)
        def _():
            pltpu.make_async_remote_copy(
                src_ref=src, dst_ref=dst, send_sem=send.at[kind, send_at], recv_sem=recv.at[kind, recv_at],
                device_id={"seq": target}, device_id_type=MESH,
            ).start()

        @pl.when(target == me)
        def _():
            dst[...] = src[...]

    def routed(kind, at, dst, origin):
        @pl.when(origin != me)
        def _():
            wait_in(kind, at, dst)

    devices = 2 * chips
    layer = lax.axis_index("dp")

    def others(count, base, body, first=1):
        def run(d, carry):
            body(lax.rem(base + d, count))
            return carry

        lax.fori_loop(first, count, run, 0)

    barrier = pltpu.get_barrier_semaphore()
    others(devices, me, lambda t: pl.semaphore_signal(barrier, inc=1, device_id={"seq": t}, device_id_type=MESH))
    others(depth, layer, lambda t: pl.semaphore_signal(barrier, inc=1, device_id={"dp": t}, device_id_type=MESH))

    logits = mm_rows(x_ref[...], w_ref[...]) + b_ref[...]
    strength[...] = 0.5 / (1.0 + jnp.exp(-logits))
    dl_s[...] = jnp.zeros_like(dl_s)
    pl.semaphore_wait(barrier, devices + depth - 2)

    def span(head):
        return pl.ds(pl.multiple_of(head * BLOCK, BLOCK), BLOCK)

    def own_head(j):
        return 2 * j + core

    def other_head(j):
        return 2 * j + 1 - core

    def local_maps(slots, heads):
        row, col = masks()
        eye = row == col
        keys = [k_ref[:, span(h)] for h in heads]
        values = [v_ref[:, span(h)] for h in heads]
        strengths = strength[...]
        lane = lax.broadcasted_iota(jnp.int32, strengths.shape, 1)
        products = [mm_rows(key, key) for key in keys]
        norms = [jnp.where(eye, product, 0.0) for product in products]
        rks = [lax.rsqrt(jnp.sum(n, axis=1, keepdims=True) + EPSILON) for n in norms]
        rkr = [lax.rsqrt(jnp.sum(n, axis=0, keepdims=True) + EPSILON) for n in norms]
        bes = [jnp.sum(jnp.where(lane == h, strengths, 0.0), axis=1, keepdims=True) for h in heads]
        ber = [jnp.sum(jnp.where(eye, be, 0.0), axis=0, keepdims=True) for be in bes]
        grams = [jnp.where(row > col, m * a * b, 0.0) for m, a, b in zip(products, rks, rkr)]
        inverses = unit_lower_inverse([g * be for g, be in zip(grams, bes)])
        weights = [x * b for x, b in zip(inverses, ber)]
        wks = [right_exact(w * r, key) for w, r, key in zip(weights, rkr, keys)]
        wvs = [right_exact(w, value) for w, value in zip(weights, values)]
        keys_t = [key.T for key in keys]
        both = [
            left_exact(kt, jnp.concatenate([a, b], axis=1) * r) for kt, a, b, r in zip(keys_t, wks, wvs, rks)
        ]
        for i, s in enumerate(slots):
            rk_col[s] = rks[i]
            be_col[s] = bes[i]
            rk_row[s] = rkr[i]
            gram_s[s] = grams[i]
            inv_s[s] = inverses[i]
            wk_s[s] = wks[i]
            wv_s[s] = wvs[i]
            key_t[s] = keys_t[i]
        eyef = eye.astype(f32)
        return [jnp.concatenate([eyef - m[:, :BLOCK], m[:, BLOCK:]], axis=1) for m in both]

    def steps(body):
        def run(r, carry):
            body([r * group + u for u in range(group)])
            return carry

        lax.fori_loop(0, rounds, run, 0)

    def first_other(js):
        made = local_maps([half + j for j in js], [other_head(j) for j in js])
        for j, m in zip(js, made):
            out_map[j] = m
        for j in js:
            push(0, j, out_map.at[j], maps.at[core, j], sibling).start()

    steps(first_other)

    def first_own(js):
        made = local_maps(js, [own_head(j) for j in js])
        for j, m in zip(js, made):
            maps[core, j] = m
        for j in js:
            wait_in(0, j, maps.at[1 - core, j])
        zero = jnp.zeros((BLOCK, BLOCK), f32)
        earlier = [maps[0, j] for j in js]
        later = [maps[1, j] for j in js]
        made = [mm3(b[:, :BLOCK], a) for a, b in zip(earlier, later)]
        for j, m, b in zip(js, made, later):
            chip_map[j] = m + jnp.concatenate([zero, b[:, BLOCK:]], axis=1)
        for j in js:
            route(1, j, place, chip_map.at[j], got_map.at[place], owner(j))

    steps(first_own)

    def score_terms(slots, heads):
        row, col = masks()
        keys = [k_ref[:, span(h)] for h in heads]
        queries = [q_ref[:, span(h)] for h in heads]
        rkr = [rk_row[s] for s in slots]
        products = [mm_rows(q, k) for q, k in zip(queries, keys)]
        wide = [q.astype(f32) for q in queries]
        rqs = [lax.rsqrt(jnp.sum(q * q, axis=1, keepdims=True) + EPSILON) for q in wide]
        ps = [jnp.where(row >= col, m * a * b, 0.0) for m, a, b in zip(products, rqs, rkr)]
        inverses_t = [inv_s[s].T for s in slots]
        zs = [right_exact(x * r, k) for x, r, k in zip(inverses_t, rkr, keys)]
        for i, s in enumerate(slots):
            rq_col[s] = rqs[i]
            p_s[s] = ps[i]
            p_t[s] = ps[i].T
            inv_t[s] = inverses_t[i]
            z_s[s] = zs[i]
            query_t[s] = queries[i].T

    steps(lambda js: score_terms(js, [own_head(j) for j in js]))
    steps(lambda js: score_terms([half + j for j in js], [other_head(j) for j in js]))

    row, col = masks()
    eyef = (row == col).astype(f32)
    zero = jnp.zeros((BLOCK, BLOCK), f32)

    slot = lax.div(chip, 2)

    @pl.when(core == 0)
    def _():
        state_out[0] = zero

        def lap(i, carry):
            routed(1, i, got_map.at[i], source(i))
            route(3, i, slot, state_out.at[i], state_in.at[slot], source(i))
            step = got_map[i]
            state_out[i + 1] = mm3(step[:, :BLOCK], state_out[i]) + step[:, BLOCK:]
            return carry

        lax.fori_loop(0, half, lap, 0)
        push(2, 0, state_out.at[half], hand_in.at[0], sibling).start()
        suffix[half] = eyef

        def back(n, carry):
            i = half - 1 - n
            turned = got_map[i][:, :BLOCK].T
            map_t[i] = turned
            suffix[i] = mm3(turned, suffix[i + 1])
            return carry

        lax.fori_loop(0, half, back, 0)

    @pl.when(core == 1)
    def _():
        prefix[0] = jnp.concatenate([eyef, zero], axis=1)

        def lap(i, carry):
            routed(1, i, got_map.at[i], source(i))
            step = got_map[i]
            map_t[i] = step[:, :BLOCK].T
            prefix[i + 1] = mm3(step[:, :BLOCK], prefix[i]) + jnp.concatenate([zero, step[:, BLOCK:]], axis=1)
            return carry

        lax.fori_loop(0, half, lap, 0)
        wait_in(2, 0, hand_in.at[0])
        entry = hand_in[0]

        def lift(r, carry):
            for u in range(group):
                i = r * group + u
                known = prefix[i]
                state_out[i] = mm3(known[:, :BLOCK], entry) + known[:, BLOCK:]
            for u in range(group):
                i = r * group + u
                route(3, i, slot, state_out.at[i], state_in.at[slot], source(i))
            return carry

        lax.fori_loop(0, rounds, lift, 0)

    def enter(j, carry):
        routed(3, j, state_in.at[j], owner(j))
        first = state_in[j]
        step = maps[0, j]
        second = mm3(step[:, :BLOCK], first) + step[:, BLOCK:]
        s_own[j] = jnp.where(core == 0, first, second)
        s_out[j] = jnp.where(core == 0, second, first)
        push(4, j, s_out.at[j], s_sib.at[j], sibling).start()
        return carry

    lax.fori_loop(0, half, enter, 0)

    def forward(slots, heads, states):
        queries = [q_ref[:, span(h)] for h in heads]
        rqs = [rq_col[s] for s in slots]
        fresh = [wv_s[s] - mm3(wk_s[s], state) for s, state in zip(slots, states)]
        read = [left_exact(q, state) * r for q, state, r in zip(queries, states, rqs)]
        outs = [o + mm3(p_s[s], f) for o, f, s in zip(read, fresh, slots)]
        outs = [o.astype(bf16) for o in outs]
        cots = [o.astype(f32) - t_ref[:, span(h)].astype(f32) for o, h in zip(outs, heads)]
        ups = [mm3(p_t[s], d) for d, s in zip(cots, slots)]
        es = [mm3(inv_t[s], u) for u, s in zip(ups, slots)]
        cs = [left_exact(query_t[s], d * r) for s, d, r in zip(slots, cots, rqs)]
        cs = [c - left_exact(key_t[s], e * (rk_col[s] * be_col[s])) for c, s, e in zip(cs, slots, es)]
        for i, (s, h) in enumerate(zip(slots, heads)):
            o_ref[:, span(h)] = outs[i]
            f_s[s] = fresh[i]
            do_s[s] = cots[i]
            e_s[s] = es[i]
        return cs

    def second_own(js):
        made = forward(js, [own_head(j) for j in js], [s_own[j] for j in js])
        for j, c in zip(js, made):
            c_both[core, j] = c

    steps(second_own)

    def second_other(js):
        for j in js:
            wait_in(4, j, s_sib.at[j])
        made = forward([half + j for j in js], [other_head(j) for j in js], [s_sib[j] for j in js])
        for j, c in zip(js, made):
            c_out[j] = c
        for j in js:
            push(5, j, c_out.at[j], c_both.at[core, j], sibling).start()

    steps(second_other)

    def join_grads(js):
        for j in js:
            wait_in(5, j, c_both.at[1 - core, j])
        made = [mm3(maps[0, j][:, :BLOCK].T, c_both[1, j]) + c_both[0, j] for j in js]
        for j, c in zip(js, made):
            c_chip[j] = c
        for j in js:
            route(6, j, place, c_chip.at[j], c_got.at[place], owner(j))

    steps(join_grads)

    def query_grads(slots, heads, states):
        row, col = masks()
        fts = [f_s[s].T for s in slots]
        sts = [state.T for state in states]
        cots = [do_s[s] for s in slots]
        rqs = [rq_col[s] for s in slots]
        dps = [jnp.where(row >= col, mm3(d, ft), 0.0) for d, ft in zip(cots, fts)]
        dqs = [mm3(d, st) for d, st in zip(cots, sts)]
        dqs = [
            d + right_exact(p * rk_row[s], k_ref[:, span(h)]) for d, p, s, h in zip(dqs, dps, slots, heads)
        ]
        turned = [right_exact((p * r).T, q_ref[:, span(h)]) for p, r, h in zip(dps, rqs, heads)]
        for i, (s, h) in enumerate(zip(slots, heads)):
            unit = q_ref[:, span(h)].astype(f32) * rqs[i]
            grad = rqs[i] * (dqs[i] - unit * jnp.sum(unit * dqs[i], axis=1, keepdims=True))
            gq_ref[:, span(h)] = grad.astype(bf16)
            dpq_s[s] = turned[i]
            f_t[s] = fts[i]
            s_t[s] = sts[i]

    steps(lambda js: query_grads(js, [own_head(j) for j in js], [s_own[j] for j in js]))
    steps(
        lambda js: query_grads(
            [half + j for j in js], [other_head(j) for j in js], [s_sib[j] for j in js]
        )
    )

    grad_out[half] = zero

    @pl.when(core == 1)
    def _():
        def lap(n, carry):
            i = half - 1 - n
            routed(6, i, c_got.at[i], source(i))
            route(8, i, slot, grad_out.at[i + 1], grad_in.at[slot], source(i))
            grad_out[i] = mm3(map_t[i], grad_out[i + 1]) + c_got[i]
            return carry

        lax.fori_loop(0, half, lap, 0)
        push(7, 0, grad_out.at[0], gh_in.at[0], sibling).start()

    @pl.when(core == 0)
    def _():
        def lap(n, carry):
            i = half - 1 - n
            routed(6, i, c_got.at[i], source(i))
            grad_out[i] = mm3(map_t[i], grad_out[i + 1]) + c_got[i]
            return carry

        lax.fori_loop(0, half, lap, 0)
        wait_in(7, 0, gh_in.at[0])
        entry = gh_in[0]

        def lift(r, carry):
            for u in range(group):
                i = half - 1 - (r * group + u)
                grad_out[i + 1] = mm3(suffix[i + 1], entry) + grad_out[i + 1]
            for u in range(group):
                i = half - 1 - (r * group + u)
                route(8, i, slot, grad_out.at[i + 1], grad_in.at[slot], source(i))
            return carry

        lax.fori_loop(0, rounds, lift, 0)

    def leave(j, carry):
        routed(8, j, grad_in.at[j], owner(j))
        last = grad_in[j]
        inner = mm3(maps[1, j][:, :BLOCK].T, last) + c_both[1, j]
        g_own[j] = jnp.where(core == 0, inner, last)
        g_out[j] = jnp.where(core == 0, last, inner)
        push(9, j, g_out.at[j], g_sib.at[j], sibling).start()
        return carry

    lax.fori_loop(0, half, leave, 0)

    def backward(slots, heads, grads):
        row, col = masks()
        es = [e_s[s] + mm3(z_s[s], g) for s, g in zip(slots, grads)]
        gts = [g.T for g in grads]
        efs = [jnp.where(row > col, mm3(e, f_t[s]), 0.0) for e, s in zip(es, slots)]
        ess = [mm3(e, s_t[s]) for e, s in zip(es, slots)]
        dks = [dpq_s[s] + mm3(f_s[s], gt) for s, gt in zip(slots, gts)]
        bes = [be_col[s] for s in slots]
        links = [ef * be for ef, be in zip(efs, bes)]
        links = [(m + m.T) * rk_row[s] for m, s in zip(links, slots)]
        dks = [d - es_ * be for d, es_, be in zip(dks, ess, bes)]
        dks = [d - right_exact(m, k_ref[:, span(h)]) for d, m, h in zip(dks, links, heads)]
        added = 0.0
        lane = lax.broadcasted_iota(jnp.int32, (BLOCK, BLOCK), 1)
        for i, (s, h) in enumerate(zip(slots, heads)):
            rk = rk_col[s]
            unit = k_ref[:, span(h)].astype(f32) * rk
            grad = rk * (dks[i] - unit * jnp.sum(unit * dks[i], axis=1, keepdims=True))
            gk_ref[:, span(h)] = grad.astype(bf16)
            gv_ref[:, span(h)] = (es[i] * bes[i]).astype(bf16)
            terms = es[i] * v_ref[:, span(h)].astype(f32) - ess[i] * unit - efs[i] * gram_s[s]
            dl = jnp.sum(terms, axis=1, keepdims=True) * (bes[i] * (1.0 - 2.0 * bes[i]))
            added = added + jnp.where(lane == s, dl, 0.0)
        dl_s[...] += added

    steps(lambda js: backward(js, [own_head(j) for j in js], [g_own[j] for j in js]))

    def gate_copy(kind, at, src, target):
        return pltpu.make_async_remote_copy(
            src_ref=src, dst_ref=(tiles if kind == 2 else gate_in).at[me], send_sem=gate_send.at[kind, at],
            recv_sem=gate_recv.at[kind // 2, me], device_id={"seq": target}, device_id_type=MESH,
        )

    def gate_wait(kind, dst, origin):
        pltpu.make_async_remote_copy(
            src_ref=dst, dst_ref=dst, send_sem=gate_send.at[kind, 0],
            recv_sem=gate_recv.at[kind, origin], device_id={"seq": sibling}, device_id_type=MESH,
        ).wait_recv()

    def gate_rows(first, tiles_ref):
        rows = dl_s[...].T[first : first + half]
        parts = jnp.concatenate([rows, rows - rows.astype(bf16).astype(f32)], axis=0).astype(bf16)
        product = mm(parts, x_ref[...])
        product = product[:half] + product[half:]
        for c in range(chips):
            tiles_ref[c] = product[:, c * BLOCK : (c + 1) * BLOCK]

    gate_rows(0, gate_own)
    gate_in[me] = gate_own[chip]
    others(chips, chip, lambda c: gate_copy(0, c, gate_own.at[c], 2 * c + core).start())

    def last_other(js):
        for j in js:
            wait_in(9, j, g_sib.at[j])
        backward([half + j for j in js], [other_head(j) for j in js], [g_sib[j] for j in js])

    steps(last_other)

    gate_rows(half, gate_other)
    others(chips, chip, lambda c: gate_copy(1, c, gate_other.at[c], 2 * c + 1 - core).start(), first=0)
    others(devices, me, lambda t: gate_wait(0, gate_in.at[t], t))
    total = gate_in[0]
    for t in range(1, devices):
        total = total + gate_in[t]
    depth_out[0] = total
    depth_in[layer] = total

    def depth_copy(t, dst):
        return pltpu.make_async_remote_copy(
            src_ref=depth_out.at[0], dst_ref=dst, send_sem=depth_send.at[t],
            recv_sem=depth_recv.at[layer], device_id={"dp": t}, device_id_type=MESH,
        )

    def depth_wait(t):
        pltpu.make_async_remote_copy(
            src_ref=depth_out.at[0], dst_ref=depth_in.at[t], send_sem=depth_send.at[t],
            recv_sem=depth_recv.at[t], device_id={"dp": t}, device_id_type=MESH,
        ).wait_recv()

    others(depth, layer, lambda t: depth_copy(t, depth_in.at[layer]).start())
    others(depth, layer, depth_wait)
    total = depth_in[0]
    for t in range(1, depth):
        total = total + depth_in[t]
    total = total * scale
    tile_out[0] = total
    tiles[me] = total
    others(devices, me, lambda t: gate_copy(2, t, tile_out.at[0], t).start())
    others(devices, me, lambda t: gate_wait(1, tiles.at[t], t))
    for t in range(devices):
        tile = tiles[t]
        for r in range(half):
            at = 2 * r + t % 2
            gw_ref[at : at + 1, (t // 2) * BLOCK : (t // 2 + 1) * BLOCK] = tile[r : r + 1]

    others(chips, chip, lambda c: gate_copy(0, c, gate_own.at[c], sibling).wait_send())
    others(chips, chip, lambda c: gate_copy(1, c, gate_other.at[c], sibling).wait_send(), first=0)
    others(depth, layer, lambda t: depth_copy(t, depth_in.at[layer]).wait_send())
    others(devices, me, lambda t: gate_copy(2, t, tile_out.at[0], sibling).wait_send())

    def drain(j, carry):
        push(0, j, out_map.at[j], out_map.at[j], sibling).wait_send()
        push(4, j, s_out.at[j], s_out.at[j], sibling).wait_send()
        push(5, j, c_out.at[j], c_out.at[j], sibling).wait_send()
        push(9, j, g_out.at[j], g_out.at[j], sibling).wait_send()

        @pl.when(owner(j) != me)
        def _():
            push(1, j, chip_map.at[j], chip_map.at[j], sibling).wait_send()
            push(6, j, c_chip.at[j], c_chip.at[j], sibling).wait_send()

        @pl.when(source(j) != me)
        def _():
            push(3, j, state_out.at[j], state_out.at[j], sibling).wait_send()
            push(8, j, grad_out.at[j + 1], grad_out.at[j + 1], sibling).wait_send()

        return carry

    lax.fori_loop(0, half, drain, 0)

    @pl.when(core == 0)
    def _():
        push(2, 0, state_out.at[half], state_out.at[half], sibling).wait_send()

    @pl.when(core == 1)
    def _():
        push(7, 0, grad_out.at[0], grad_out.at[0], sibling).wait_send()


def shards(chips, depth, queries, keys_in, values_in, inputs, target, gate_weight, beta_bias):
    heads = gate_weight.shape[1]
    width = heads * BLOCK
    half = heads // 2
    square = (BLOCK, BLOCK)

    def many(count, *tail, kind=f32):
        return pltpu.VMEM((count,) + (tail or square), kind)

    wide = (BLOCK, 2 * BLOCK)
    scratch = [
        pltpu.VMEM((BLOCK, heads), f32), many(heads, BLOCK, 1), many(heads, BLOCK, 1), many(heads, BLOCK, 1),
        many(heads, 1, BLOCK),
        many(heads, kind=bf16), many(heads, kind=bf16),
    ] + [many(heads)] * 8 + [many(heads)] * 6 + [
        pltpu.VMEM(square, f32),
        pltpu.VMEM((2, half) + wide, f32), many(half, *wide), many(half, *wide), many(half, *wide),
        many(half + 1, *wide), many(half + 1), many(1), many(half), many(half), many(half), many(half),
        pltpu.VMEM((2, half) + square, f32), many(half), many(half), many(half), many(half + 1), many(half),
        many(half + 1), many(1), many(half), many(half), many(half), many(half),
        many(chips, half, BLOCK), many(chips, half, BLOCK), many(2 * chips, half, BLOCK), many(1, half, BLOCK),
        many(depth, half, BLOCK), many(1, half, BLOCK), many(2 * chips, half, BLOCK),
        pltpu.SemaphoreType.DMA((10, half)), pltpu.SemaphoreType.DMA((10, half)),
        pltpu.SemaphoreType.DMA((3, 2 * chips)), pltpu.SemaphoreType.DMA((2, 2 * chips)),
        pltpu.SemaphoreType.DMA((depth,)), pltpu.SemaphoreType.DMA((depth,)),
    ]
    rows = jax.ShapeDtypeStruct((BLOCK, width), bf16)
    whole = pl.BlockSpec(memory_space=pltpu.VMEM)
    results = pl.pallas_call(
        functools.partial(kernel, chips, depth, 1.0 / math.sqrt(BLOCK * 2 * chips * depth)),
        out_shape=(rows, rows, rows, rows, jax.ShapeDtypeStruct((heads, inputs.shape[-1]), f32)),
        in_specs=[whole] * 7,
        out_specs=(whole,) * 5,
        scratch_shapes=scratch,
        compiler_params=pltpu.CompilerParams(
            collective_id=0, has_side_effects=True, vmem_limit_bytes=52 * 1024 * 1024
        ),
    )(queries[0], keys_in[0], values_in[0], inputs[0], target[0], gate_weight.T, beta_bias[None])
    output, grad_q, grad_k, grad_v, grad_w = results
    return (output[None], grad_q[None], grad_k[None], grad_v[None], grad_w.T)


def solution(mesh):
    placed = P("dp", "seq", None)
    chips = mesh.shape["seq"] // 2
    return jax.shard_map(
        functools.partial(shards, chips, mesh.shape["dp"]),
        mesh=mesh,
        in_specs=(placed,) * 5 + (P(), P()),
        out_specs=(placed,) * 4 + (P(),),
        check_vma=False,
    )
```

```python
import functools
import math

import jax
import jax.numpy as jnp
from jax import lax
from jax.experimental import pallas as pl
from jax.experimental.pallas import tpu as pltpu
from jax.sharding import PartitionSpec as P

BLOCK = 128
EPSILON = 1e-06
GROUP = 8
f32 = jnp.float32
bf16 = jnp.bfloat16
MESH = pl.DeviceIdType.MESH


def mm(a, b):
    return jnp.dot(a, b, preferred_element_type=f32)


def mm_rows(a, b):
    return lax.dot_general(a, b, (((1,), (1,)), ((), ())), preferred_element_type=f32)


def mm3(a, b):
    return jnp.dot(a, b, preferred_element_type=f32, precision=lax.Precision.HIGH)


def split(x):
    high = x.astype(bf16)
    return high, (x - high.astype(f32)).astype(bf16)


def left_exact(exact, x):
    high, low = split(x)
    return mm(exact, high) + mm(exact, low)


def right_exact(x, exact):
    high, low = split(x)
    return mm(high, exact) + mm(low, exact)


def masks():
    row = lax.broadcasted_iota(jnp.int32, (BLOCK, BLOCK), 0)
    col = lax.broadcasted_iota(jnp.int32, (BLOCK, BLOCK), 1)
    return row, col


def unit_lower_inverse(systems):
    row, col = masks()
    apart = row ^ col
    eye = (row == col).astype(f32)
    inverses = [eye - jnp.where(apart < 2, a, 0.0) for a in systems]
    size = 2
    while size < BLOCK:
        band = (apart >= size) & (apart < 2 * size)
        packed = [x.astype(bf16) for x in inverses]
        steps = [mm(jnp.where(band, a, 0.0).astype(bf16), x) for a, x in zip(systems, packed)]
        steps = [mm(x, y.astype(bf16)) for x, y in zip(packed, steps)]
        inverses = [x - y for x, y in zip(inverses, steps)]
        size *= 2
    rest = [mm3(a, x) for a, x in zip(systems, inverses)]
    rest = [(eye - x - y) for x, y in zip(inverses, rest)]
    fixes = [mm(x.astype(bf16), y.astype(bf16)) for x, y in zip(inverses, rest)]
    return [x + y for x, y in zip(inverses, fixes)]


def kernel(
    chips, depth, scale,
    q_ref, k_ref, v_ref, x_ref, t_ref, w_ref, b_ref,
    o_ref, gq_ref, gk_ref, gv_ref, gw_ref,
    strength, rk_col, rq_col, be_col, rk_row,
    key_t, query_t, gram_s, inv_s, inv_t, wk_s, wv_s, p_s, p_t, z_s,
    f_s, f_t, s_t, do_s, e_s, dpq_s, dl_s,
    maps, out_map, chip_map, got_map, prefix, state_out, hand_in, state_in, s_own, s_sib, s_out,
    c_both, c_out, c_chip, c_got, suffix, map_t, grad_out, gh_in, grad_in, g_own, g_sib, g_out,
    gate_out, gate_in, column_out, column_in, depth_out, depth_in, tile_out, tiles,
    send, recv, gate_send, gate_recv,
):
    me = lax.axis_index("seq")
    core = lax.rem(me, 2)
    chip = lax.div(me, 2)
    half = chips // 2
    part = lax.div(chip, half)
    place = lax.rem(chip, half)
    parity = lax.rem(chip, 2)
    sibling = me + 1 - 2 * core
    rounds = half // min(GROUP, half)
    group = min(GROUP, half)

    def owner(j):
        return 2 * (2 * j + core) + part

    def source(i):
        return 2 * (half * core + i) + parity

    def push(kind, at, src, dst, target):
        return pltpu.make_async_remote_copy(
            src_ref=src, dst_ref=dst, send_sem=send.at[kind, at], recv_sem=recv.at[kind, at],
            device_id={"seq": target}, device_id_type=MESH,
        )

    def wait_in(kind, at, dst):
        push(kind, at, dst, dst, sibling).wait_recv()

    def route(kind, send_at, recv_at, src, dst, target):
        @pl.when(target != me)
        def _():
            pltpu.make_async_remote_copy(
                src_ref=src, dst_ref=dst, send_sem=send.at[kind, send_at], recv_sem=recv.at[kind, recv_at],
                device_id={"seq": target}, device_id_type=MESH,
            ).start()

        @pl.when(target == me)
        def _():
            dst[...] = src[...]

    def routed(kind, at, dst, origin):
        @pl.when(origin != me)
        def _():
            wait_in(kind, at, dst)

    devices = 2 * chips
    layer = lax.axis_index("dp")

    def others(count, base, body, first=1):
        def run(d, carry):
            body(lax.rem(base + d, count))
            return carry

        lax.fori_loop(first, count, run, 0)

    barrier = pltpu.get_barrier_semaphore()
    others(devices, me, lambda t: pl.semaphore_signal(barrier, inc=1, device_id={"seq": t}, device_id_type=MESH))
    others(depth, layer, lambda t: pl.semaphore_signal(barrier, inc=1, device_id={"dp": t}, device_id_type=MESH))

    logits = mm_rows(x_ref[...], w_ref[...]) + b_ref[...]
    strength[...] = 0.5 / (1.0 + jnp.exp(-logits))
    dl_s[...] = jnp.zeros_like(dl_s)

    def span(head):
        return pl.ds(pl.multiple_of(head * BLOCK, BLOCK), BLOCK)

    def own_head(j):
        return 2 * j + core

    def other_head(j):
        return 2 * j + 1 - core

    def local_maps(slots, heads):
        row, col = masks()
        eye = row == col
        keys = [k_ref[:, span(h)] for h in heads]
        values = [v_ref[:, span(h)] for h in heads]
        strengths = strength[...]
        lane = lax.broadcasted_iota(jnp.int32, strengths.shape, 1)
        products = [mm_rows(key, key) for key in keys]
        norms = [jnp.where(eye, product, 0.0) for product in products]
        rks = [lax.rsqrt(jnp.sum(n, axis=1, keepdims=True) + EPSILON) for n in norms]
        rkr = [lax.rsqrt(jnp.sum(n, axis=0, keepdims=True) + EPSILON) for n in norms]
        bes = [jnp.sum(jnp.where(lane == h, strengths, 0.0), axis=1, keepdims=True) for h in heads]
        ber = [jnp.sum(jnp.where(eye, be, 0.0), axis=0, keepdims=True) for be in bes]
        grams = [jnp.where(row > col, m * a * b, 0.0) for m, a, b in zip(products, rks, rkr)]
        inverses = unit_lower_inverse([g * be for g, be in zip(grams, bes)])
        weights = [x * b for x, b in zip(inverses, ber)]
        wks = [right_exact(w * r, key) for w, r, key in zip(weights, rkr, keys)]
        wvs = [right_exact(w, value) for w, value in zip(weights, values)]
        keys_t = [key.T for key in keys]
        both = [
            left_exact(kt, jnp.concatenate([a, b], axis=1) * r) for kt, a, b, r in zip(keys_t, wks, wvs, rks)
        ]
        for i, s in enumerate(slots):
            rk_col[s] = rks[i]
            be_col[s] = bes[i]
            rk_row[s] = rkr[i]
            gram_s[s] = grams[i]
            inv_s[s] = inverses[i]
            wk_s[s] = wks[i]
            wv_s[s] = wvs[i]
            key_t[s] = keys_t[i]
        eyef = eye.astype(f32)
        return [jnp.concatenate([eyef - m[:, :BLOCK], m[:, BLOCK:]], axis=1) for m in both]

    def steps(body):
        def run(r, carry):
            body([r * group + u for u in range(group)])
            return carry

        lax.fori_loop(0, rounds, run, 0)

    def first(js):
        slots = [half + j for j in js] + list(js)
        heads = [other_head(j) for j in js] + [own_head(j) for j in js]
        made = local_maps(slots, heads)
        for i, j in enumerate(js):
            out_map[j] = made[i]
            maps[core, j] = made[len(js) + i]
        return slots, heads

    def compose_maps(js):
        for j in js:
            wait_in(0, j, maps.at[1 - core, j])
        nothing = jnp.zeros((BLOCK, BLOCK), f32)
        earlier = [maps[0, j] for j in js]
        later = [maps[1, j] for j in js]
        made = [mm3(b[:, :BLOCK], a) for a, b in zip(earlier, later)]
        for j, m, b in zip(js, made, later):
            chip_map[j] = m + jnp.concatenate([nothing, b[:, BLOCK:]], axis=1)
        for j in js:
            route(1, j, place, chip_map.at[j], got_map.at[place], owner(j))

    def score_terms(slots, heads):
        row, col = masks()
        keys = [k_ref[:, span(h)] for h in heads]
        queries = [q_ref[:, span(h)] for h in heads]
        rkr = [rk_row[s] for s in slots]
        products = [mm_rows(q, k) for q, k in zip(queries, keys)]
        wide = [q.astype(f32) for q in queries]
        rqs = [lax.rsqrt(jnp.sum(q * q, axis=1, keepdims=True) + EPSILON) for q in wide]
        ps = [jnp.where(row >= col, m * a * b, 0.0) for m, a, b in zip(products, rqs, rkr)]
        inverses_t = [inv_s[s].T for s in slots]
        zs = [right_exact(x * r, k) for x, r, k in zip(inverses_t, rkr, keys)]
        for i, s in enumerate(slots):
            rq_col[s] = rqs[i]
            p_s[s] = ps[i]
            p_t[s] = ps[i].T
            inv_t[s] = inverses_t[i]
            z_s[s] = zs[i]
            query_t[s] = queries[i].T

    for r in range(2):
        js = range(r * half // 2, (r + 1) * half // 2)
        slots, heads = first(js)
        if r == 0:
            pl.semaphore_wait(barrier, devices + depth - 2)
        for j in js:
            push(0, j, out_map.at[j], maps.at[core, j], sibling).start()
        score_terms(slots, heads)
        compose_maps(js)

    row, col = masks()
    eyef = (row == col).astype(f32)
    zero = jnp.zeros((BLOCK, BLOCK), f32)

    slot = lax.div(chip, 2)

    @pl.when(core == 0)
    def _():
        state_out[0] = zero

        def lap(i, carry):
            routed(1, i, got_map.at[i], source(i))
            route(3, i, slot, state_out.at[i], state_in.at[slot], source(i))
            step = got_map[i]
            state_out[i + 1] = mm3(step[:, :BLOCK], state_out[i]) + step[:, BLOCK:]
            return carry

        lax.fori_loop(0, half, lap, 0)
        push(2, 0, state_out.at[half], hand_in.at[0], sibling).start()
        suffix[half] = eyef

        def back(n, carry):
            i = half - 1 - n
            turned = got_map[i][:, :BLOCK].T
            map_t[i] = turned
            suffix[i] = mm3(turned, suffix[i + 1])
            return carry

        lax.fori_loop(0, half, back, 0)

    @pl.when(core == 1)
    def _():
        prefix[0] = jnp.concatenate([eyef, zero], axis=1)

        def lap(i, carry):
            routed(1, i, got_map.at[i], source(i))
            step = got_map[i]
            map_t[i] = step[:, :BLOCK].T
            prefix[i + 1] = mm3(step[:, :BLOCK], prefix[i]) + jnp.concatenate([zero, step[:, BLOCK:]], axis=1)
            return carry

        lax.fori_loop(0, half, lap, 0)
        wait_in(2, 0, hand_in.at[0])
        entry = hand_in[0]

        def lift(r, carry):
            for u in range(group):
                i = r * group + u
                known = prefix[i]
                state_out[i] = mm3(known[:, :BLOCK], entry) + known[:, BLOCK:]
            for u in range(group):
                i = r * group + u
                route(3, i, slot, state_out.at[i], state_in.at[slot], source(i))
            return carry

        lax.fori_loop(0, rounds, lift, 0)

    def enter(j, carry):
        routed(3, j, state_in.at[j], owner(j))
        first = state_in[j]
        step = maps[0, j]
        second = mm3(step[:, :BLOCK], first) + step[:, BLOCK:]
        s_own[j] = jnp.where(core == 0, first, second)
        s_out[j] = jnp.where(core == 0, second, first)
        push(4, j, s_out.at[j], s_sib.at[j], sibling).start()
        return carry

    lax.fori_loop(0, half, enter, 0)

    def forward(slots, heads, states):
        queries = [q_ref[:, span(h)] for h in heads]
        rqs = [rq_col[s] for s in slots]
        fresh = [wv_s[s] - mm3(wk_s[s], state) for s, state in zip(slots, states)]
        read = [left_exact(q, state) * r for q, state, r in zip(queries, states, rqs)]
        outs = [o + mm3(p_s[s], f) for o, f, s in zip(read, fresh, slots)]
        outs = [o.astype(bf16) for o in outs]
        cots = [o.astype(f32) - t_ref[:, span(h)].astype(f32) for o, h in zip(outs, heads)]
        ups = [mm3(p_t[s], d) for d, s in zip(cots, slots)]
        es = [mm3(inv_t[s], u) for u, s in zip(ups, slots)]
        cs = [left_exact(query_t[s], d * r) for s, d, r in zip(slots, cots, rqs)]
        cs = [c - left_exact(key_t[s], e * (rk_col[s] * be_col[s])) for c, s, e in zip(cs, slots, es)]
        for i, (s, h) in enumerate(zip(slots, heads)):
            o_ref[:, span(h)] = outs[i]
            f_s[s] = fresh[i]
            do_s[s] = cots[i]
            e_s[s] = es[i]
        return cs

    def second_own(js):
        made = forward(js, [own_head(j) for j in js], [s_own[j] for j in js])
        for j, c in zip(js, made):
            c_both[core, j] = c

    steps(second_own)

    def second_other(js):
        for j in js:
            wait_in(4, j, s_sib.at[j])
        made = forward([half + j for j in js], [other_head(j) for j in js], [s_sib[j] for j in js])
        for j, c in zip(js, made):
            c_out[j] = c
        for j in js:
            push(5, j, c_out.at[j], c_both.at[core, j], sibling).start()

    steps(second_other)

    def join_grads(js):
        for j in js:
            wait_in(5, j, c_both.at[1 - core, j])
        made = [mm3(maps[0, j][:, :BLOCK].T, c_both[1, j]) + c_both[0, j] for j in js]
        for j, c in zip(js, made):
            c_chip[j] = c
        for j in js:
            route(6, j, place, c_chip.at[j], c_got.at[place], owner(j))

    steps(join_grads)

    def query_grads(slots, heads, states):
        row, col = masks()
        fts = [f_s[s].T for s in slots]
        sts = [state.T for state in states]
        cots = [do_s[s] for s in slots]
        rqs = [rq_col[s] for s in slots]
        dps = [jnp.where(row >= col, mm3(d, ft), 0.0) for d, ft in zip(cots, fts)]
        dqs = [mm3(d, st) for d, st in zip(cots, sts)]
        dqs = [
            d + right_exact(p * rk_row[s], k_ref[:, span(h)]) for d, p, s, h in zip(dqs, dps, slots, heads)
        ]
        turned = [right_exact((p * r).T, q_ref[:, span(h)]) for p, r, h in zip(dps, rqs, heads)]
        for i, (s, h) in enumerate(zip(slots, heads)):
            unit = q_ref[:, span(h)].astype(f32) * rqs[i]
            grad = rqs[i] * (dqs[i] - unit * jnp.sum(unit * dqs[i], axis=1, keepdims=True))
            gq_ref[:, span(h)] = grad.astype(bf16)
            dpq_s[s] = turned[i]
            f_t[s] = fts[i]
            s_t[s] = sts[i]

    steps(lambda js: query_grads(js, [own_head(j) for j in js], [s_own[j] for j in js]))
    steps(
        lambda js: query_grads(
            [half + j for j in js], [other_head(j) for j in js], [s_sib[j] for j in js]
        )
    )

    grad_out[half] = zero

    @pl.when(core == 1)
    def _():
        def lap(n, carry):
            i = half - 1 - n
            routed(6, i, c_got.at[i], source(i))
            route(8, i, slot, grad_out.at[i + 1], grad_in.at[slot], source(i))
            grad_out[i] = mm3(map_t[i], grad_out[i + 1]) + c_got[i]
            return carry

        lax.fori_loop(0, half, lap, 0)
        push(7, 0, grad_out.at[0], gh_in.at[0], sibling).start()

    @pl.when(core == 0)
    def _():
        def lap(n, carry):
            i = half - 1 - n
            routed(6, i, c_got.at[i], source(i))
            grad_out[i] = mm3(map_t[i], grad_out[i + 1]) + c_got[i]
            return carry

        lax.fori_loop(0, half, lap, 0)
        wait_in(7, 0, gh_in.at[0])
        entry = gh_in[0]

        def lift(r, carry):
            for u in range(group):
                i = half - 1 - (r * group + u)
                grad_out[i + 1] = mm3(suffix[i + 1], entry) + grad_out[i + 1]
            for u in range(group):
                i = half - 1 - (r * group + u)
                route(8, i, slot, grad_out.at[i + 1], grad_in.at[slot], source(i))
            return carry

        lax.fori_loop(0, rounds, lift, 0)

    def leave(j, carry):
        routed(8, j, grad_in.at[j], owner(j))
        last = grad_in[j]
        inner = mm3(maps[1, j][:, :BLOCK].T, last) + c_both[1, j]
        g_own[j] = jnp.where(core == 0, inner, last)
        g_out[j] = jnp.where(core == 0, last, inner)
        push(9, j, g_out.at[j], g_sib.at[j], sibling).start()
        return carry

    lax.fori_loop(0, half, leave, 0)

    def gate_terms(slots, heads, grads):
        row, col = masks()
        es = [e_s[s] + mm3(z_s[s], g) for s, g in zip(slots, grads)]
        efs = [jnp.where(row > col, mm3(e, f_t[s]), 0.0) for e, s in zip(es, slots)]
        ess = [mm3(e, s_t[s]) for e, s in zip(es, slots)]
        added = 0.0
        lane = lax.broadcasted_iota(jnp.int32, (BLOCK, BLOCK), 1)
        for i, (s, h) in enumerate(zip(slots, heads)):
            be = be_col[s]
            unit = k_ref[:, span(h)].astype(f32) * rk_col[s]
            gv_ref[:, span(h)] = (es[i] * be).astype(bf16)
            terms = es[i] * v_ref[:, span(h)].astype(f32) - ess[i] * unit - efs[i] * gram_s[s]
            dl = jnp.sum(terms, axis=1, keepdims=True) * (be * (1.0 - 2.0 * be))
            added = added + jnp.where(lane == s, dl, 0.0)
            p_s[s] = efs[i]
            p_t[s] = ess[i]
        dl_s[...] += added

    def key_grads(slots, heads, grads):
        gts = [g.T for g in grads]
        bes = [be_col[s] for s in slots]
        dks = [dpq_s[s] + mm3(f_s[s], gt) for s, gt in zip(slots, gts)]
        links = [p_s[s] * be for s, be in zip(slots, bes)]
        links = [(m + m.T) * rk_row[s] for m, s in zip(links, slots)]
        dks = [d - p_t[s] * be for d, s, be in zip(dks, slots, bes)]
        dks = [d - right_exact(m, k_ref[:, span(h)]) for d, m, h in zip(dks, links, heads)]
        for i, (s, h) in enumerate(zip(slots, heads)):
            rk = rk_col[s]
            unit = k_ref[:, span(h)].astype(f32) * rk
            grad = rk * (dks[i] - unit * jnp.sum(unit * dks[i], axis=1, keepdims=True))
            gk_ref[:, span(h)] = grad.astype(bf16)

    side = 2 ** (chips.bit_length() // 2)
    column, line = lax.div(chip, side), lax.rem(chip, side)
    start = column * (2 * side)
    at_row = 2 * line + core
    in_row = (2 * side, at_row, lambda i: {"seq": start + i})
    in_column = (chips // side, column, lambda i: {"seq": (i * side + line) * 2 + core})
    in_depth = (depth, layer, lambda i: {"dp": i})

    def swap(kind, ring, src, dst):
        count, here, target = ring
        made = []
        for d in range(1, count):
            i = lax.rem(here + d, count)
            copy = pltpu.make_async_remote_copy(
                src_ref=src(i), dst_ref=dst.at[here], send_sem=gate_send.at[kind, i],
                recv_sem=gate_recv.at[kind, here], device_id=target(i), device_id_type=MESH,
            )
            copy.start()
            made.append(copy)
        return made

    def summed(kind, ring, dst):
        arrive(kind, ring, dst)
        total = dst[0]
        for i in range(1, ring[0]):
            total = total + dst[i]
        return total

    def arrive(kind, ring, dst):
        count, here, target = ring
        for d in range(1, count):
            i = lax.rem(here + d, count)
            pltpu.make_async_remote_copy(
                src_ref=dst.at[i], dst_ref=dst.at[i], send_sem=gate_send.at[kind, i],
                recv_sem=gate_recv.at[kind, i], device_id=target(i), device_id_type=MESH,
            ).wait_recv()

    steps(lambda js: gate_terms(js, [own_head(j) for j in js], [g_own[j] for j in js]))

    def last_other(js):
        for j in js:
            wait_in(9, j, g_sib.at[j])
        gate_terms([half + j for j in js], [other_head(j) for j in js], [g_sib[j] for j in js])

    steps(last_other)

    rows = dl_s[...].T[: 2 * half]
    parts = jnp.concatenate([rows, rows - rows.astype(bf16).astype(f32)], axis=0).astype(bf16)
    product = mm(parts, x_ref[...])
    product = product[: 2 * half] + product[2 * half :]
    width = gate_out.shape[-1]
    for y in range(side):
        gate_out[2 * y + core] = product[:half, y * width : (y + 1) * width]
        gate_out[2 * y + 1 - core] = product[half:, y * width : (y + 1) * width]
    gate_in[at_row] = gate_out[at_row]
    copies = swap(0, in_row, lambda i: gate_out.at[i], gate_in)
    steps(lambda js: key_grads(js, [own_head(j) for j in js], [g_own[j] for j in js]))
    total = summed(0, in_row, gate_in)
    column_out[0] = total
    column_in[column] = total
    copies += swap(1, in_column, lambda i: column_out.at[0], column_in)
    steps(lambda js: key_grads([half + j for j in js], [other_head(j) for j in js], [g_sib[j] for j in js]))
    total = summed(1, in_column, column_in)
    depth_out[0] = total
    depth_in[layer] = total
    copies += swap(2, in_depth, lambda i: depth_out.at[0], depth_in)
    total = summed(2, in_depth, depth_in) * scale
    tile_out[0] = total
    tiles[at_row] = total
    copies += swap(3, in_row, lambda i: tile_out.at[0], tiles)
    arrive(3, in_row, tiles)
    for t in range(2 * side):
        tile = tiles[t]
        for r in range(half):
            at = 2 * r + t % 2
            gw_ref[at : at + 1, (t // 2) * width : (t // 2 + 1) * width] = tile[r : r + 1]
    for copy in copies:
        copy.wait_send()

    def drain(j, carry):
        push(0, j, out_map.at[j], out_map.at[j], sibling).wait_send()
        push(4, j, s_out.at[j], s_out.at[j], sibling).wait_send()
        push(5, j, c_out.at[j], c_out.at[j], sibling).wait_send()
        push(9, j, g_out.at[j], g_out.at[j], sibling).wait_send()

        @pl.when(owner(j) != me)
        def _():
            push(1, j, chip_map.at[j], chip_map.at[j], sibling).wait_send()
            push(6, j, c_chip.at[j], c_chip.at[j], sibling).wait_send()

        @pl.when(source(j) != me)
        def _():
            push(3, j, state_out.at[j], state_out.at[j], sibling).wait_send()
            push(8, j, grad_out.at[j + 1], grad_out.at[j + 1], sibling).wait_send()

        return carry

    lax.fori_loop(0, half, drain, 0)

    @pl.when(core == 0)
    def _():
        push(2, 0, state_out.at[half], state_out.at[half], sibling).wait_send()

    @pl.when(core == 1)
    def _():
        push(7, 0, grad_out.at[0], grad_out.at[0], sibling).wait_send()


def publish(*refs):
    copies = [pltpu.make_async_copy(refs[i], refs[5 + i], refs[10].at[i]) for i in range(5)]
    for copy in copies:
        copy.start()
    for copy in copies:
        copy.wait()


def shards(chips, depth, queries, keys_in, values_in, inputs, target, gate_weight, beta_bias):
    heads = gate_weight.shape[1]
    width = heads * BLOCK
    half = heads // 2
    square = (BLOCK, BLOCK)

    def many(count, *tail, kind=f32):
        return pltpu.VMEM((count,) + (tail or square), kind)

    wide = (BLOCK, 2 * BLOCK)
    side = 2 ** (chips.bit_length() // 2)
    cut = inputs.shape[-1] // side
    scratch = [
        pltpu.VMEM((BLOCK, heads), f32), many(heads, BLOCK, 1), many(heads, BLOCK, 1), many(heads, BLOCK, 1),
        many(heads, 1, BLOCK),
        many(heads, kind=bf16), many(heads, kind=bf16),
    ] + [many(heads)] * 8 + [many(heads)] * 6 + [
        pltpu.VMEM(square, f32),
        pltpu.VMEM((2, half) + wide, f32), many(half, *wide), many(half, *wide), many(half, *wide),
        many(half + 1, *wide), many(half + 1), many(1), many(half), many(half), many(half), many(half),
        pltpu.VMEM((2, half) + square, f32), many(half), many(half), many(half), many(half + 1), many(half),
        many(half + 1), many(1), many(half), many(half), many(half), many(half),
        many(2 * side, half, cut), many(2 * side, half, cut), many(1, half, cut), many(chips // side, half, cut),
        many(1, half, cut), many(depth, half, cut), many(1, half, cut), many(2 * side, half, cut),
        pltpu.SemaphoreType.DMA((10, half)), pltpu.SemaphoreType.DMA((10, half)),
        pltpu.SemaphoreType.DMA((4, 16)), pltpu.SemaphoreType.DMA((4, 16)),
    ]
    rows = jax.ShapeDtypeStruct((BLOCK, width), bf16)
    whole = pl.BlockSpec(memory_space=pltpu.VMEM)
    results = pl.pallas_call(
        functools.partial(kernel, chips, depth, 1.0 / math.sqrt(BLOCK * 2 * chips * depth)),
        out_shape=(rows, rows, rows, rows, jax.ShapeDtypeStruct((heads, inputs.shape[-1]), f32)),
        in_specs=[whole] * 7,
        out_specs=(whole,) * 5,
        scratch_shapes=scratch,
        compiler_params=pltpu.CompilerParams(
            collective_id=0, has_side_effects=True, vmem_limit_bytes=52 * 1024 * 1024
        ),
    )(queries[0], keys_in[0], values_in[0], inputs[0], target[0], gate_weight.T, beta_bias[None])
    anywhere = pl.BlockSpec(memory_space=pl.ANY)
    output, grad_q, grad_k, grad_v, grad_w = pl.pallas_call(
        publish,
        out_shape=tuple(jax.ShapeDtypeStruct(r.shape, r.dtype) for r in results),
        in_specs=[anywhere] * 5,
        out_specs=(anywhere,) * 5,
        scratch_shapes=[pltpu.SemaphoreType.DMA((5,))],
        compiler_params=pltpu.CompilerParams(vmem_limit_bytes=1024 * 1024),
    )(*results)
    return (output[None], grad_q[None], grad_k[None], grad_v[None], grad_w.T)


def solution(mesh):
    placed = P("dp", "seq", None)
    chips = mesh.shape["seq"] // 2
    return jax.shard_map(
        functools.partial(shards, chips, mesh.shape["dp"]),
        mesh=mesh,
        in_specs=(placed,) * 5 + (P(), P()),
        out_specs=(placed,) * 4 + (P(),),
        check_vma=False,
    )
```

```python
import functools
import math

import jax
import jax.numpy as jnp
from jax import lax
from jax.experimental import pallas as pl
from jax.experimental.pallas import tpu as pltpu
from jax.sharding import PartitionSpec as P

BLOCK = 128
EPSILON = 1e-06
GROUP = 8
f32 = jnp.float32
bf16 = jnp.bfloat16
MESH = pl.DeviceIdType.MESH


def mm(a, b):
    return jnp.dot(a, b, preferred_element_type=f32)


def mm_rows(a, b):
    return lax.dot_general(a, b, (((1,), (1,)), ((), ())), preferred_element_type=f32)


def mm3(a, b):
    return jnp.dot(a, b, preferred_element_type=f32, precision=lax.Precision.HIGH)


def split(x):
    high = x.astype(bf16)
    return high, (x - high.astype(f32)).astype(bf16)


def left_exact(exact, x):
    high, low = split(x)
    return mm(exact, high) + mm(exact, low)


def right_exact(x, exact):
    high, low = split(x)
    return mm(high, exact) + mm(low, exact)


def masks():
    row = lax.broadcasted_iota(jnp.int32, (BLOCK, BLOCK), 0)
    col = lax.broadcasted_iota(jnp.int32, (BLOCK, BLOCK), 1)
    return row, col


def unit_lower_inverse(systems):
    row, col = masks()
    apart = row ^ col
    eye = (row == col).astype(f32)
    inverses = [eye - jnp.where(apart < 2, a, 0.0) for a in systems]
    size = 2
    while size < BLOCK:
        band = (apart >= size) & (apart < 2 * size)
        packed = [x.astype(bf16) for x in inverses]
        steps = [mm(jnp.where(band, a, 0.0).astype(bf16), x) for a, x in zip(systems, packed)]
        steps = [mm(x, y.astype(bf16)) for x, y in zip(packed, steps)]
        inverses = [x - y for x, y in zip(inverses, steps)]
        size *= 2
    rest = [mm3(a, x) for a, x in zip(systems, inverses)]
    rest = [(eye - x - y) for x, y in zip(inverses, rest)]
    fixes = [mm(x.astype(bf16), y.astype(bf16)) for x, y in zip(inverses, rest)]
    return [x + y for x, y in zip(inverses, fixes)]


def kernel(
    chips, depth, scale,
    q_ref, k_ref, v_ref, x_ref, t_ref, w_ref, b_ref,
    o_ref, gq_ref, gk_ref, gv_ref, gw_ref,
    strength, rk_col, rq_col, be_col, rk_row,
    key_t, query_t, gram_s, inv_s, inv_t, wk_s, wv_s, p_s, p_t, z_s,
    early_t, late_t, f_s, f_t, s_t, do_s, e_s, dpq_s, dl_s,
    maps, out_map, chip_map, got_map, prefix, state_out, hand_in, state_in, s_own, s_sib, s_out,
    c_both, c_out, c_chip, c_got, suffix, map_t, grad_out, gh_in, grad_in, g_own, g_sib, g_out,
    gate_out, gate_in, column_out, column_in, depth_out, depth_in, tile_out, tiles,
    send, recv, gate_send, gate_recv,
):
    me = lax.axis_index("seq")
    core = lax.rem(me, 2)
    chip = lax.div(me, 2)
    half = chips // 2
    part = lax.div(chip, half)
    place = lax.rem(chip, half)
    across, along = lax.div(chip, 4), lax.rem(chip, 4)
    spread = chips == 16
    mine = 8 * lax.rem(across + along, 2) + 2 * across + lax.div(along, 2) if spread else chip
    parity = lax.rem(mine, 2)
    sibling = me + 1 - 2 * core
    rounds = half // min(GROUP, half)
    group = min(GROUP, half)

    def owner(j):
        head = 2 * j + core
        if spread:
            bank, seat = lax.div(head, 8), lax.rem(head, 8)
            line = lax.div(seat, 2)
            head = 4 * line + 2 * lax.rem(seat, 2) + lax.rem(line + bank, 2)
        return 2 * head + part

    def source(i):
        return 2 * (half * core + i) + parity

    def push(kind, at, src, dst, target):
        return pltpu.make_async_remote_copy(
            src_ref=src, dst_ref=dst, send_sem=send.at[kind, at], recv_sem=recv.at[kind, at],
            device_id={"seq": target}, device_id_type=MESH,
        )

    def wait_in(kind, at, dst):
        push(kind, at, dst, dst, sibling).wait_recv()

    def route(kind, send_at, recv_at, src, dst, target):
        @pl.when(target != me)
        def _():
            pltpu.make_async_remote_copy(
                src_ref=src, dst_ref=dst, send_sem=send.at[kind, send_at], recv_sem=recv.at[kind, recv_at],
                device_id={"seq": target}, device_id_type=MESH,
            ).start()

        @pl.when(target == me)
        def _():
            dst[...] = src[...]

    def routed(kind, at, dst, origin):
        @pl.when(origin != me)
        def _():
            wait_in(kind, at, dst)

    devices = 2 * chips
    layer = lax.axis_index("dp")

    def others(count, base, body, first=1):
        def run(d, carry):
            body(lax.rem(base + d, count))
            return carry

        lax.fori_loop(first, count, run, 0)

    barrier = pltpu.get_barrier_semaphore()
    others(devices, me, lambda t: pl.semaphore_signal(barrier, inc=1, device_id={"seq": t}, device_id_type=MESH))
    others(depth, layer, lambda t: pl.semaphore_signal(barrier, inc=1, device_id={"dp": t}, device_id_type=MESH))

    logits = mm_rows(x_ref[...], w_ref[...]) + b_ref[...]
    strength[...] = 0.5 / (1.0 + jnp.exp(-logits))
    dl_s[...] = jnp.zeros_like(dl_s)

    def span(head):
        return pl.ds(pl.multiple_of(head * BLOCK, BLOCK), BLOCK)

    def own_head(j):
        return 2 * j + core

    def other_head(j):
        return 2 * j + 1 - core

    def local_maps(slots, heads):
        row, col = masks()
        eye = row == col
        keys = [k_ref[:, span(h)] for h in heads]
        values = [v_ref[:, span(h)] for h in heads]
        strengths = strength[...]
        lane = lax.broadcasted_iota(jnp.int32, strengths.shape, 1)
        products = [mm_rows(key, key) for key in keys]
        norms = [jnp.where(eye, product, 0.0) for product in products]
        rks = [lax.rsqrt(jnp.sum(n, axis=1, keepdims=True) + EPSILON) for n in norms]
        rkr = [lax.rsqrt(jnp.sum(n, axis=0, keepdims=True) + EPSILON) for n in norms]
        bes = [jnp.sum(jnp.where(lane == h, strengths, 0.0), axis=1, keepdims=True) for h in heads]
        ber = [jnp.sum(jnp.where(eye, be, 0.0), axis=0, keepdims=True) for be in bes]
        grams = [jnp.where(row > col, m * a * b, 0.0) for m, a, b in zip(products, rks, rkr)]
        inverses = unit_lower_inverse([g * be for g, be in zip(grams, bes)])
        weights = [x * b for x, b in zip(inverses, ber)]
        wks = [right_exact(w * r, key) for w, r, key in zip(weights, rkr, keys)]
        wvs = [right_exact(w, value) for w, value in zip(weights, values)]
        keys_t = [key.T for key in keys]
        both = [
            left_exact(kt, jnp.concatenate([a, b], axis=1) * r) for kt, a, b, r in zip(keys_t, wks, wvs, rks)
        ]
        for i, s in enumerate(slots):
            rk_col[s] = rks[i]
            be_col[s] = bes[i]
            rk_row[s] = rkr[i]
            gram_s[s] = grams[i]
            inv_s[s] = inverses[i]
            wk_s[s] = wks[i]
            wv_s[s] = wvs[i]
            key_t[s] = keys_t[i]
        eyef = eye.astype(f32)
        return [jnp.concatenate([eyef - m[:, :BLOCK], m[:, BLOCK:]], axis=1) for m in both]

    def first(js):
        slots = [half + j for j in js] + list(js)
        heads = [other_head(j) for j in js] + [own_head(j) for j in js]
        made = local_maps(slots, heads)
        for i, j in enumerate(js):
            out_map[j] = made[i]
            maps[core, j] = made[len(js) + i]
        return slots, heads

    def compose_maps(js):
        for j in js:
            wait_in(0, j, maps.at[1 - core, j])
        nothing = jnp.zeros((BLOCK, BLOCK), f32)
        earlier = [maps[0, j] for j in js]
        later = [maps[1, j] for j in js]
        made = [mm3(b[:, :BLOCK], a) for a, b in zip(earlier, later)]
        for j, m, b in zip(js, made, later):
            chip_map[j] = m + jnp.concatenate([nothing, b[:, BLOCK:]], axis=1)
        for j in js:
            route(1, j, place, chip_map.at[j], got_map.at[place], owner(j))

    def score_terms(slots, heads):
        row, col = masks()
        keys = [k_ref[:, span(h)] for h in heads]
        queries = [q_ref[:, span(h)] for h in heads]
        rkr = [rk_row[s] for s in slots]
        products = [mm_rows(q, k) for q, k in zip(queries, keys)]
        wide = [q.astype(f32) for q in queries]
        rqs = [lax.rsqrt(jnp.sum(q * q, axis=1, keepdims=True) + EPSILON) for q in wide]
        ps = [jnp.where(row >= col, m * a * b, 0.0) for m, a, b in zip(products, rqs, rkr)]
        inverses_t = [inv_s[s].T for s in slots]
        zs = [right_exact(x * r, k) for x, r, k in zip(inverses_t, rkr, keys)]
        for i, s in enumerate(slots):
            rq_col[s] = rqs[i]
            p_s[s] = ps[i]
            p_t[s] = ps[i].T
            inv_t[s] = inverses_t[i]
            z_s[s] = zs[i]
            query_t[s] = queries[i].T

    for r in range(2):
        js = range(r * half // 2, (r + 1) * half // 2)
        slots, heads = first(js)
        if r == 0:
            pl.semaphore_wait(barrier, devices + depth - 2)
        for j in js:
            push(0, j, out_map.at[j], maps.at[core, j], sibling).start()
        score_terms(slots, heads)
        compose_maps(js)

    row, col = masks()
    eyef = (row == col).astype(f32)
    zero = jnp.zeros((BLOCK, BLOCK), f32)

    slot = lax.div(mine, 2)

    @pl.when(core == 0)
    def _():
        state_out[0] = zero

        def lap(i, carry):
            routed(1, i, got_map.at[i], source(i))
            route(3, i, slot, state_out.at[i], state_in.at[slot], source(i))
            step = got_map[i]
            state_out[i + 1] = mm3(step[:, :BLOCK], state_out[i]) + step[:, BLOCK:]
            return carry

        lax.fori_loop(0, half, lap, 0)
        push(2, 0, state_out.at[half], hand_in.at[0], sibling).start()
        suffix[half] = eyef

        def back(n, carry):
            i = half - 1 - n
            turned = got_map[i][:, :BLOCK].T
            map_t[i] = turned
            suffix[i] = mm3(turned, suffix[i + 1])
            return carry

        lax.fori_loop(0, half, back, 0)

    @pl.when(core == 1)
    def _():
        prefix[0] = jnp.concatenate([eyef, zero], axis=1)

        def lap(i, carry):
            routed(1, i, got_map.at[i], source(i))
            step = got_map[i]
            map_t[i] = step[:, :BLOCK].T
            prefix[i + 1] = mm3(step[:, :BLOCK], prefix[i]) + jnp.concatenate([zero, step[:, BLOCK:]], axis=1)
            return carry

        lax.fori_loop(0, half, lap, 0)
        wait_in(2, 0, hand_in.at[0])
        entry = hand_in[0]

        def lift(r, carry):
            for u in range(group):
                i = r * group + u
                known = prefix[i]
                state_out[i] = mm3(known[:, :BLOCK], entry) + known[:, BLOCK:]
            for u in range(group):
                i = r * group + u
                route(3, i, slot, state_out.at[i], state_in.at[slot], source(i))
            return carry

        lax.fori_loop(0, rounds, lift, 0)

    for j in range(half):
        early_t[j] = maps[0, j][:, :BLOCK].T
        late_t[j] = maps[1, j][:, :BLOCK].T

    def enter(js):
        for j in js:
            routed(3, j, state_in.at[j], owner(j))
        firsts = [state_in[j] for j in js]
        steps_ = [maps[0, j] for j in js]
        seconds = [mm3(m[:, :BLOCK], a) + m[:, BLOCK:] for m, a in zip(steps_, firsts)]
        for j, a, b in zip(js, firsts, seconds):
            s_own[j] = jnp.where(core == 0, a, b)
            s_out[j] = jnp.where(core == 0, b, a)
        for j in js:
            push(4, j, s_out.at[j], s_sib.at[j], sibling).start()

    def forward(slots, heads, states):
        queries = [q_ref[:, span(h)] for h in heads]
        rqs = [rq_col[s] for s in slots]
        fresh = [wv_s[s] - mm3(wk_s[s], state) for s, state in zip(slots, states)]
        read = [left_exact(q, state) * r for q, state, r in zip(queries, states, rqs)]
        outs = [o + mm3(p_s[s], f) for o, f, s in zip(read, fresh, slots)]
        outs = [o.astype(bf16) for o in outs]
        cots = [o.astype(f32) - t_ref[:, span(h)].astype(f32) for o, h in zip(outs, heads)]
        ups = [mm3(p_t[s], d) for d, s in zip(cots, slots)]
        es = [mm3(inv_t[s], u) for u, s in zip(ups, slots)]
        cs = [left_exact(query_t[s], d * r) for s, d, r in zip(slots, cots, rqs)]
        cs = [c - left_exact(key_t[s], e * (rk_col[s] * be_col[s])) for c, s, e in zip(cs, slots, es)]
        for i, (s, h) in enumerate(zip(slots, heads)):
            o_ref[:, span(h)] = outs[i]
            f_s[s] = fresh[i]
            do_s[s] = cots[i]
            e_s[s] = es[i]
        return cs

    def join_grads(js):
        for j in js:
            wait_in(5, j, c_both.at[1 - core, j])
        made = [mm3(early_t[j], c_both[1, j]) + c_both[0, j] for j in js]
        for j, c in zip(js, made):
            c_chip[j] = c
        for j in js:
            route(6, j, place, c_chip.at[j], c_got.at[place], owner(j))

    def query_grads(slots, heads, states):
        row, col = masks()
        fts = [f_s[s].T for s in slots]
        sts = [state.T for state in states]
        cots = [do_s[s] for s in slots]
        rqs = [rq_col[s] for s in slots]
        dps = [jnp.where(row >= col, mm3(d, ft), 0.0) for d, ft in zip(cots, fts)]
        dqs = [mm3(d, st) for d, st in zip(cots, sts)]
        dqs = [
            d + right_exact(p * rk_row[s], k_ref[:, span(h)]) for d, p, s, h in zip(dqs, dps, slots, heads)
        ]
        turned = [right_exact((p * r).T, q_ref[:, span(h)]) for p, r, h in zip(dps, rqs, heads)]
        for i, (s, h) in enumerate(zip(slots, heads)):
            unit = q_ref[:, span(h)].astype(f32) * rqs[i]
            grad = rqs[i] * (dqs[i] - unit * jnp.sum(unit * dqs[i], axis=1, keepdims=True))
            gq_ref[:, span(h)] = grad.astype(bf16)
            dpq_s[s] = turned[i]
            f_t[s] = fts[i]
            s_t[s] = sts[i]

    def both(body, js, ours, theirs):
        slots = list(js) + [half + j for j in js]
        heads = [own_head(j) for j in js] + [other_head(j) for j in js]
        return body(slots, heads, [ours[j] for j in js] + [theirs[j] for j in js])

    for r in range(2):
        js = range(r * half // 2, (r + 1) * half // 2)
        enter(js)
        for j in js:
            wait_in(4, j, s_sib.at[j])
        made = both(forward, js, s_own, s_sib)
        for i, j in enumerate(js):
            c_both[core, j] = made[i]
            c_out[j] = made[len(js) + i]
        for j in js:
            push(5, j, c_out.at[j], c_both.at[core, j], sibling).start()
        if r == 0:
            both(query_grads, js, s_own, s_sib)
        join_grads(js)
    both(query_grads, js, s_own, s_sib)

    def drain_early(j, carry):
        push(0, j, out_map.at[j], out_map.at[j], sibling).wait_send()
        push(4, j, s_out.at[j], s_out.at[j], sibling).wait_send()
        push(5, j, c_out.at[j], c_out.at[j], sibling).wait_send()

        @pl.when(owner(j) != me)
        def _():
            push(1, j, chip_map.at[j], chip_map.at[j], sibling).wait_send()

        @pl.when(source(j) != me)
        def _():
            push(3, j, state_out.at[j], state_out.at[j], sibling).wait_send()

        return carry

    @pl.when(core == 0)
    def _():
        push(2, 0, state_out.at[half], state_out.at[half], sibling).wait_send()

    grad_out[half] = zero

    @pl.when(core == 1)
    def _():
        def lap(n, carry):
            i = half - 1 - n
            routed(6, i, c_got.at[i], source(i))
            route(8, i, slot, grad_out.at[i + 1], grad_in.at[slot], source(i))
            grad_out[i] = mm3(map_t[i], grad_out[i + 1]) + c_got[i]
            return carry

        lax.fori_loop(0, half, lap, 0)
        push(7, 0, grad_out.at[0], gh_in.at[0], sibling).start()

    @pl.when(core == 0)
    def _():
        def lap(n, carry):
            i = half - 1 - n
            routed(6, i, c_got.at[i], source(i))
            grad_out[i] = mm3(map_t[i], grad_out[i + 1]) + c_got[i]
            return carry

        lax.fori_loop(0, half, lap, 0)
        wait_in(7, 0, gh_in.at[0])
        entry = gh_in[0]

        def lift(r, carry):
            for u in range(group):
                i = half - 1 - (r * group + u)
                grad_out[i + 1] = mm3(suffix[i + 1], entry) + grad_out[i + 1]
            for u in range(group):
                i = half - 1 - (r * group + u)
                route(8, i, slot, grad_out.at[i + 1], grad_in.at[slot], source(i))
            return carry

        lax.fori_loop(0, rounds, lift, 0)

    lax.fori_loop(0, half, drain_early, 0)

    def leave(js):
        for j in js:
            routed(8, j, grad_in.at[j], owner(j))
        lasts = [grad_in[j] for j in js]
        inners = [mm3(late_t[j], g) + c_both[1, j] for j, g in zip(js, lasts)]
        for j, a, b in zip(js, lasts, inners):
            g_own[j] = jnp.where(core == 0, b, a)
            g_out[j] = jnp.where(core == 0, a, b)
        for j in js:
            push(9, j, g_out.at[j], g_sib.at[j], sibling).start()

    def gate_terms(slots, heads, grads):
        row, col = masks()
        es = [e_s[s] + mm3(z_s[s], g) for s, g in zip(slots, grads)]
        efs = [jnp.where(row > col, mm3(e, f_t[s]), 0.0) for e, s in zip(es, slots)]
        ess = [mm3(e, s_t[s]) for e, s in zip(es, slots)]
        added = 0.0
        lane = lax.broadcasted_iota(jnp.int32, (BLOCK, BLOCK), 1)
        for i, (s, h) in enumerate(zip(slots, heads)):
            be = be_col[s]
            unit = k_ref[:, span(h)].astype(f32) * rk_col[s]
            gv_ref[:, span(h)] = (es[i] * be).astype(bf16)
            terms = es[i] * v_ref[:, span(h)].astype(f32) - ess[i] * unit - efs[i] * gram_s[s]
            dl = jnp.sum(terms, axis=1, keepdims=True) * (be * (1.0 - 2.0 * be))
            added = added + jnp.where(lane == s, dl, 0.0)
            p_s[s] = efs[i]
            p_t[s] = ess[i]
        dl_s[...] += added

    def key_grads(slots, heads, grads):
        gts = [g.T for g in grads]
        bes = [be_col[s] for s in slots]
        dks = [dpq_s[s] + mm3(f_s[s], gt) for s, gt in zip(slots, gts)]
        links = [p_s[s] * be for s, be in zip(slots, bes)]
        links = [(m + m.T) * rk_row[s] for m, s in zip(links, slots)]
        dks = [d - p_t[s] * be for d, s, be in zip(dks, slots, bes)]
        dks = [d - right_exact(m, k_ref[:, span(h)]) for d, m, h in zip(dks, links, heads)]
        for i, (s, h) in enumerate(zip(slots, heads)):
            rk = rk_col[s]
            unit = k_ref[:, span(h)].astype(f32) * rk
            grad = rk * (dks[i] - unit * jnp.sum(unit * dks[i], axis=1, keepdims=True))
            gk_ref[:, span(h)] = grad.astype(bf16)

    side = 2 ** (chips.bit_length() // 2)
    column, line = lax.div(chip, side), lax.rem(chip, side)
    start = column * (2 * side)
    at_row = 2 * line + core
    in_row = (2 * side, at_row, lambda i: {"seq": start + i})
    in_column = (chips // side, column, lambda i: {"seq": (i * side + line) * 2 + core})
    in_depth = (depth, layer, lambda i: {"dp": i})

    def swap(kind, ring, src, dst):
        count, here, target = ring
        made = []
        for d in range(1, count):
            i = lax.rem(here + d, count)
            copy = pltpu.make_async_remote_copy(
                src_ref=src(i), dst_ref=dst.at[here], send_sem=gate_send.at[kind, i],
                recv_sem=gate_recv.at[kind, here], device_id=target(i), device_id_type=MESH,
            )
            copy.start()
            made.append(copy)
        return made

    def summed(kind, ring, dst):
        arrive(kind, ring, dst)
        total = dst[0]
        for i in range(1, ring[0]):
            total = total + dst[i]
        return total

    def arrive(kind, ring, dst):
        count, here, target = ring
        for d in range(1, count):
            i = lax.rem(here + d, count)
            pltpu.make_async_remote_copy(
                src_ref=dst.at[i], dst_ref=dst.at[i], send_sem=gate_send.at[kind, i],
                recv_sem=gate_recv.at[kind, i], device_id=target(i), device_id_type=MESH,
            ).wait_recv()

    for r in range(2):
        js = range(r * half // 2, (r + 1) * half // 2)
        leave(js)
        for j in js:
            wait_in(9, j, g_sib.at[j])
        both(gate_terms, js, g_own, g_sib)

    rows = dl_s[...].T[: 2 * half]
    parts = jnp.concatenate([rows, rows - rows.astype(bf16).astype(f32)], axis=0).astype(bf16)
    product = mm(parts, x_ref[...])
    product = product[: 2 * half] + product[2 * half :]
    width = gate_out.shape[-1]
    for y in range(side):
        gate_out[2 * y + core] = product[:half, y * width : (y + 1) * width]
        gate_out[2 * y + 1 - core] = product[half:, y * width : (y + 1) * width]
    gate_in[at_row] = gate_out[at_row]
    copies = swap(0, in_row, lambda i: gate_out.at[i], gate_in)
    both(key_grads, range(half // 2), g_own, g_sib)
    total = summed(0, in_row, gate_in)
    column_out[0] = total
    column_in[column] = total
    copies += swap(1, in_column, lambda i: column_out.at[0], column_in)
    both(key_grads, range(half // 2, half), g_own, g_sib)
    total = summed(1, in_column, column_in)
    depth_out[0] = total
    depth_in[layer] = total
    copies += swap(2, in_depth, lambda i: depth_out.at[0], depth_in)

    def drain_late(j, carry):
        push(9, j, g_out.at[j], g_out.at[j], sibling).wait_send()

        @pl.when(owner(j) != me)
        def _():
            push(6, j, c_chip.at[j], c_chip.at[j], sibling).wait_send()

        @pl.when(source(j) != me)
        def _():
            push(8, j, grad_out.at[j + 1], grad_out.at[j + 1], sibling).wait_send()

        return carry

    lax.fori_loop(0, half, drain_late, 0)

    @pl.when(core == 1)
    def _():
        push(7, 0, grad_out.at[0], grad_out.at[0], sibling).wait_send()

    total = summed(2, in_depth, depth_in) * scale
    tile_out[0] = total
    tiles[at_row] = total
    last = swap(3, in_row, lambda i: tile_out.at[0], tiles)
    for copy in copies:
        copy.wait_send()
    arrive(3, in_row, tiles)
    for t in range(2 * side):
        tile = tiles[t]
        for r in range(half):
            at = 2 * r + t % 2
            gw_ref[at : at + 1, (t // 2) * width : (t // 2 + 1) * width] = tile[r : r + 1]
    for copy in last:
        copy.wait_send()


def publish(*refs):
    copies = [pltpu.make_async_copy(refs[i], refs[5 + i], refs[10].at[i]) for i in range(5)]
    for copy in copies:
        copy.start()
    for copy in copies:
        copy.wait()


def shards(chips, depth, queries, keys_in, values_in, inputs, target, gate_weight, beta_bias):
    heads = gate_weight.shape[1]
    width = heads * BLOCK
    half = heads // 2
    square = (BLOCK, BLOCK)

    def many(count, *tail, kind=f32):
        return pltpu.VMEM((count,) + (tail or square), kind)

    wide = (BLOCK, 2 * BLOCK)
    side = 2 ** (chips.bit_length() // 2)
    cut = inputs.shape[-1] // side
    scratch = [
        pltpu.VMEM((BLOCK, heads), f32), many(heads, BLOCK, 1), many(heads, BLOCK, 1), many(heads, BLOCK, 1),
        many(heads, 1, BLOCK),
        many(heads, kind=bf16), many(heads, kind=bf16),
    ] + [many(heads)] * 8 + [many(half)] * 2 + [many(heads)] * 6 + [
        pltpu.VMEM(square, f32),
        pltpu.VMEM((2, half) + wide, f32), many(half, *wide), many(half, *wide), many(half, *wide),
        many(half + 1, *wide), many(half + 1), many(1), many(half), many(half), many(half), many(half),
        pltpu.VMEM((2, half) + square, f32), many(half), many(half), many(half), many(half + 1), many(half),
        many(half + 1), many(1), many(half), many(half), many(half), many(half),
        many(2 * side, half, cut), many(2 * side, half, cut), many(1, half, cut), many(chips // side, half, cut),
        many(1, half, cut), many(depth, half, cut), many(1, half, cut), many(2 * side, half, cut),
        pltpu.SemaphoreType.DMA((10, half)), pltpu.SemaphoreType.DMA((10, half)),
        pltpu.SemaphoreType.DMA((4, 16)), pltpu.SemaphoreType.DMA((4, 16)),
    ]
    rows = jax.ShapeDtypeStruct((BLOCK, width), bf16)
    whole = pl.BlockSpec(memory_space=pltpu.VMEM)
    results = pl.pallas_call(
        functools.partial(kernel, chips, depth, 1.0 / math.sqrt(BLOCK * 2 * chips * depth)),
        out_shape=(rows, rows, rows, rows, jax.ShapeDtypeStruct((heads, inputs.shape[-1]), f32)),
        in_specs=[whole] * 7,
        out_specs=(whole,) * 5,
        scratch_shapes=scratch,
        compiler_params=pltpu.CompilerParams(
            collective_id=0, has_side_effects=True, vmem_limit_bytes=52 * 1024 * 1024
        ),
    )(queries[0], keys_in[0], values_in[0], inputs[0], target[0], gate_weight.T, beta_bias[None])
    anywhere = pl.BlockSpec(memory_space=pl.ANY)
    output, grad_q, grad_k, grad_v, grad_w = pl.pallas_call(
        publish,
        out_shape=tuple(jax.ShapeDtypeStruct(r.shape, r.dtype) for r in results),
        in_specs=[anywhere] * 5,
        out_specs=(anywhere,) * 5,
        scratch_shapes=[pltpu.SemaphoreType.DMA((5,))],
        compiler_params=pltpu.CompilerParams(vmem_limit_bytes=1024 * 1024),
    )(*results)
    return (output[None], grad_q[None], grad_k[None], grad_v[None], grad_w.T)


def solution(mesh):
    placed = P("dp", "seq", None)
    chips = mesh.shape["seq"] // 2
    return jax.shard_map(
        functools.partial(shards, chips, mesh.shape["dp"]),
        mesh=mesh,
        in_specs=(placed,) * 5 + (P(), P()),
        out_specs=(placed,) * 4 + (P(),),
        check_vma=False,
    )
```

```python
import functools
import math

import jax
import jax.numpy as jnp
from jax import lax
from jax.experimental import pallas as pl
from jax.experimental.pallas import tpu as pltpu
from jax.sharding import PartitionSpec as P

BLOCK = 128
EPSILON = 1e-06
GROUP = 8
f32 = jnp.float32
bf16 = jnp.bfloat16
MESH = pl.DeviceIdType.MESH


def mm(a, b):
    return jnp.dot(a, b, preferred_element_type=f32)


def mm_rows(a, b):
    return lax.dot_general(a, b, (((1,), (1,)), ((), ())), preferred_element_type=f32)


def mm3(a, b):
    return jnp.dot(a, b, preferred_element_type=f32, precision=lax.Precision.HIGH)


def mm3_rows(a, b):
    return lax.dot_general(a, b, (((1,), (1,)), ((), ())), preferred_element_type=f32, precision=lax.Precision.HIGH)


def split(x):
    high = x.astype(bf16)
    return high, (x - high.astype(f32)).astype(bf16)


def left_exact(exact, x):
    high, low = split(x)
    return mm(exact, high) + mm(exact, low)


def right_exact(x, exact):
    high, low = split(x)
    return mm(high, exact) + mm(low, exact)


def masks():
    row = lax.broadcasted_iota(jnp.int32, (BLOCK, BLOCK), 0)
    col = lax.broadcasted_iota(jnp.int32, (BLOCK, BLOCK), 1)
    return row, col


def unit_lower_inverse(systems):
    row, col = masks()
    apart = row ^ col
    eye = (row == col).astype(f32)
    inverses = [eye - jnp.where(apart < 2, a, 0.0) for a in systems]
    size = 2
    while size < BLOCK:
        band = (apart >= size) & (apart < 2 * size)
        packed = [x.astype(bf16) for x in inverses]
        steps = [mm(jnp.where(band, a, 0.0).astype(bf16), x) for a, x in zip(systems, packed)]
        steps = [mm(x, y.astype(bf16)) for x, y in zip(packed, steps)]
        inverses = [x - y for x, y in zip(inverses, steps)]
        size *= 2
    rest = [mm3(a, x) for a, x in zip(systems, inverses)]
    rest = [(eye - x - y) for x, y in zip(inverses, rest)]
    fixes = [mm(x.astype(bf16), y.astype(bf16)) for x, y in zip(inverses, rest)]
    return [x + y for x, y in zip(inverses, fixes)]


def kernel(
    chips, depth, scale,
    q_ref, k_ref, v_ref, x_ref, t_ref, w_ref, b_ref,
    o_ref, gq_ref, gk_ref, gv_ref, gw_ref,
    strength, rk_col, rq_col, be_col, rk_row,
    key_t, query_t, gram_s, inv_s, inv_t, wk_s, wv_s, p_s, p_t, z_s,
    early_t, late_t, f_s, f_t, s_t, do_s, e_s, dpq_s, dl_s,
    maps, out_map, chip_map, got_map, prefix, state_out, hand_in, state_in, s_own, s_sib, s_out,
    c_both, c_out, c_chip, c_got, suffix, map_t, grad_out, gh_in, grad_in, g_own, g_sib, g_out,
    gate_out, gate_in, column_out, column_in, depth_out, depth_in, tile_out, tiles,
    send, recv, gate_send, gate_recv,
):
    me = lax.axis_index("seq")
    core = lax.rem(me, 2)
    chip = lax.div(me, 2)
    half = chips // 2
    part = lax.div(chip, half)
    place = lax.rem(chip, half)
    across, along = lax.div(chip, 4), lax.rem(chip, 4)
    spread = chips == 16
    mine = 8 * lax.rem(across + along, 2) + 2 * across + lax.div(along, 2) if spread else chip
    parity = lax.rem(mine, 2)
    sibling = me + 1 - 2 * core
    rounds = half // min(GROUP, half)
    group = min(GROUP, half)

    def owner(j):
        head = 2 * j + core
        if spread:
            bank, seat = lax.div(head, 8), lax.rem(head, 8)
            line = lax.div(seat, 2)
            head = 4 * line + 2 * lax.rem(seat, 2) + lax.rem(line + bank, 2)
        return 2 * head + part

    def source(i):
        return 2 * (half * core + i) + parity

    def push(kind, at, src, dst, target):
        return pltpu.make_async_remote_copy(
            src_ref=src, dst_ref=dst, send_sem=send.at[kind, at], recv_sem=recv.at[kind, at],
            device_id={"seq": target}, device_id_type=MESH,
        )

    def wait_in(kind, at, dst):
        push(kind, at, dst, dst, sibling).wait_recv()

    def route(kind, send_at, recv_at, src, dst, target):
        @pl.when(target != me)
        def _():
            pltpu.make_async_remote_copy(
                src_ref=src, dst_ref=dst, send_sem=send.at[kind, send_at], recv_sem=recv.at[kind, recv_at],
                device_id={"seq": target}, device_id_type=MESH,
            ).start()

        @pl.when(target == me)
        def _():
            dst[...] = src[...]

    def routed(kind, at, dst, origin):
        @pl.when(origin != me)
        def _():
            wait_in(kind, at, dst)

    devices = 2 * chips
    layer = lax.axis_index("dp")

    def others(count, base, body, first=1):
        def run(d, carry):
            body(lax.rem(base + d, count))
            return carry

        lax.fori_loop(first, count, run, 0)

    barrier = pltpu.get_barrier_semaphore()
    others(devices, me, lambda t: pl.semaphore_signal(barrier, inc=1, device_id={"seq": t}, device_id_type=MESH))
    others(depth, layer, lambda t: pl.semaphore_signal(barrier, inc=1, device_id={"dp": t}, device_id_type=MESH))

    logits = mm_rows(x_ref[...], w_ref[...]) + b_ref[...]
    strength[...] = 0.5 / (1.0 + jnp.exp(-logits))
    dl_s[...] = jnp.zeros_like(dl_s)

    def span(head):
        return pl.ds(pl.multiple_of(head * BLOCK, BLOCK), BLOCK)

    def own_head(j):
        return 2 * j + core

    def other_head(j):
        return 2 * j + 1 - core

    def local_maps(slots, heads):
        row, col = masks()
        eye = row == col
        keys = [k_ref[:, span(h)] for h in heads]
        values = [v_ref[:, span(h)] for h in heads]
        strengths = strength[...]
        lane = lax.broadcasted_iota(jnp.int32, strengths.shape, 1)
        products = [mm_rows(key, key) for key in keys]
        norms = [jnp.where(eye, product, 0.0) for product in products]
        rks = [lax.rsqrt(jnp.sum(n, axis=1, keepdims=True) + EPSILON) for n in norms]
        rkr = [lax.rsqrt(jnp.sum(n, axis=0, keepdims=True) + EPSILON) for n in norms]
        bes = [jnp.sum(jnp.where(lane == h, strengths, 0.0), axis=1, keepdims=True) for h in heads]
        ber = [jnp.sum(jnp.where(eye, be, 0.0), axis=0, keepdims=True) for be in bes]
        grams = [jnp.where(row > col, m * a * b, 0.0) for m, a, b in zip(products, rks, rkr)]
        inverses = unit_lower_inverse([g * be for g, be in zip(grams, bes)])
        weights = [x * b for x, b in zip(inverses, ber)]
        wks = [right_exact(w * r, key) for w, r, key in zip(weights, rkr, keys)]
        wvs = [right_exact(w, value) for w, value in zip(weights, values)]
        keys_t = [key.T for key in keys]
        both = [
            left_exact(kt, jnp.concatenate([a, b], axis=1) * r) for kt, a, b, r in zip(keys_t, wks, wvs, rks)
        ]
        for i, s in enumerate(slots):
            rk_col[s] = rks[i]
            be_col[s] = bes[i]
            rk_row[s] = rkr[i]
            gram_s[s] = grams[i]
            inv_s[s] = inverses[i]
            wk_s[s] = wks[i]
            wv_s[s] = wvs[i]
            key_t[s] = keys_t[i]
        eyef = eye.astype(f32)
        return [jnp.concatenate([eyef - m[:, :BLOCK], m[:, BLOCK:]], axis=1) for m in both]

    def first(js):
        slots = [half + j for j in js] + list(js)
        heads = [other_head(j) for j in js] + [own_head(j) for j in js]
        made = local_maps(slots, heads)
        for i, j in enumerate(js):
            out_map[j] = made[i]
            maps[core, j] = made[len(js) + i]
        return slots, heads

    def compose_maps(js):
        for j in js:
            wait_in(0, j, maps.at[1 - core, j])
        nothing = jnp.zeros((BLOCK, BLOCK), f32)
        earlier = [maps[0, j] for j in js]
        later = [maps[1, j] for j in js]
        made = [mm3(b[:, :BLOCK], a) for a, b in zip(earlier, later)]
        for j, m, b in zip(js, made, later):
            chip_map[j] = m + jnp.concatenate([nothing, b[:, BLOCK:]], axis=1)
        for j in js:
            route(1, j, place, chip_map.at[j], got_map.at[place], owner(j))

    def score_terms(slots, heads):
        row, col = masks()
        keys = [k_ref[:, span(h)] for h in heads]
        queries = [q_ref[:, span(h)] for h in heads]
        rkr = [rk_row[s] for s in slots]
        products = [mm_rows(q, k) for q, k in zip(queries, keys)]
        wide = [q.astype(f32) for q in queries]
        rqs = [lax.rsqrt(jnp.sum(q * q, axis=1, keepdims=True) + EPSILON) for q in wide]
        ps = [jnp.where(row >= col, m * a * b, 0.0) for m, a, b in zip(products, rqs, rkr)]
        inverses_t = [inv_s[s].T for s in slots]
        zs = [right_exact(x * r, k) for x, r, k in zip(inverses_t, rkr, keys)]
        for i, s in enumerate(slots):
            rq_col[s] = rqs[i]
            p_s[s] = ps[i]
            p_t[s] = ps[i].T
            inv_t[s] = inverses_t[i]
            z_s[s] = zs[i]
            query_t[s] = queries[i].T

    for r in range(2):
        js = range(r * half // 2, (r + 1) * half // 2)
        slots, heads = first(js)
        if r == 0:
            pl.semaphore_wait(barrier, devices + depth - 2)
        for j in js:
            push(0, j, out_map.at[j], maps.at[core, j], sibling).start()
        score_terms(slots, heads)
        compose_maps(js)

    row, col = masks()
    eyef = (row == col).astype(f32)
    zero = jnp.zeros((BLOCK, BLOCK), f32)

    slot = lax.div(mine, 2)

    @pl.when(core == 0)
    def _():
        state_out[0] = zero
        turned_state = None
        for r in range(2):
            here = range(r * half // 2, (r + 1) * half // 2)
            for i in here:
                routed(1, i, got_map.at[i], source(i))
            for i in here:
                step = got_map[i]
                if turned_state is None:
                    turned_state = step[:, BLOCK:].T
                else:
                    turned_state = mm3_rows(turned_state, step[:, :BLOCK]) + step[:, BLOCK:].T
                state_out[i + 1] = turned_state.T
            for i in here:
                route(3, i, slot, state_out.at[i], state_in.at[slot], source(i))
        push(2, 0, state_out.at[half], hand_in.at[0], sibling).start()
        suffix[half] = eyef

        def back(n, carry):
            i = half - 1 - n
            turned = got_map[i][:, :BLOCK].T
            map_t[i] = turned
            suffix[i] = mm3(turned, suffix[i + 1])
            return carry

        lax.fori_loop(0, half, back, 0)

    @pl.when(core == 1)
    def _():
        prefix[0] = jnp.concatenate([eyef, zero], axis=1)

        def lap(i, carry):
            routed(1, i, got_map.at[i], source(i))
            step = got_map[i]
            map_t[i] = step[:, :BLOCK].T
            prefix[i + 1] = mm3(step[:, :BLOCK], prefix[i]) + jnp.concatenate([zero, step[:, BLOCK:]], axis=1)
            return carry

        lax.fori_loop(0, half, lap, 0)
        wait_in(2, 0, hand_in.at[0])
        entry = hand_in[0]

        def lift(r, carry):
            for u in range(group):
                i = r * group + u
                known = prefix[i]
                state_out[i] = mm3(known[:, :BLOCK], entry) + known[:, BLOCK:]
            for u in range(group):
                i = r * group + u
                route(3, i, slot, state_out.at[i], state_in.at[slot], source(i))
            return carry

        lax.fori_loop(0, rounds, lift, 0)

    for j in range(half):
        early_t[j] = maps[0, j][:, :BLOCK].T
        late_t[j] = maps[1, j][:, :BLOCK].T

    def enter(js):
        for j in js:
            routed(3, j, state_in.at[j], owner(j))
        firsts = [state_in[j] for j in js]
        steps_ = [maps[0, j] for j in js]
        seconds = [mm3(m[:, :BLOCK], a) + m[:, BLOCK:] for m, a in zip(steps_, firsts)]
        for j, a, b in zip(js, firsts, seconds):
            s_own[j] = jnp.where(core == 0, a, b)
            s_out[j] = jnp.where(core == 0, b, a)
        for j in js:
            push(4, j, s_out.at[j], s_sib.at[j], sibling).start()

    def forward(slots, heads, states):
        queries = [q_ref[:, span(h)] for h in heads]
        rqs = [rq_col[s] for s in slots]
        fresh = [wv_s[s] - mm3(wk_s[s], state) for s, state in zip(slots, states)]
        read = [left_exact(q, state) * r for q, state, r in zip(queries, states, rqs)]
        outs = [o + mm3(p_s[s], f) for o, f, s in zip(read, fresh, slots)]
        outs = [o.astype(bf16) for o in outs]
        cots = [o.astype(f32) - t_ref[:, span(h)].astype(f32) for o, h in zip(outs, heads)]
        ups = [mm3(p_t[s], d) for d, s in zip(cots, slots)]
        es = [mm3(inv_t[s], u) for u, s in zip(ups, slots)]
        cs = [left_exact(query_t[s], d * r) for s, d, r in zip(slots, cots, rqs)]
        cs = [c - left_exact(key_t[s], e * (rk_col[s] * be_col[s])) for c, s, e in zip(cs, slots, es)]
        for i, (s, h) in enumerate(zip(slots, heads)):
            o_ref[:, span(h)] = outs[i]
            f_s[s] = fresh[i]
            do_s[s] = cots[i]
            e_s[s] = es[i]
        return cs

    def join_grads(js):
        for j in js:
            wait_in(5, j, c_both.at[1 - core, j])
        made = [mm3(early_t[j], c_both[1, j]) + c_both[0, j] for j in js]
        for j, c in zip(js, made):
            c_chip[j] = c
        for j in js:
            route(6, j, place, c_chip.at[j], c_got.at[place], owner(j))

    def query_grads(slots, heads, states):
        row, col = masks()
        fts = [f_s[s].T for s in slots]
        sts = [state.T for state in states]
        cots = [do_s[s] for s in slots]
        rqs = [rq_col[s] for s in slots]
        dps = [jnp.where(row >= col, mm3(d, ft), 0.0) for d, ft in zip(cots, fts)]
        dqs = [mm3(d, st) for d, st in zip(cots, sts)]
        dqs = [
            d + right_exact(p * rk_row[s], k_ref[:, span(h)]) for d, p, s, h in zip(dqs, dps, slots, heads)
        ]
        turned = [right_exact((p * r).T, q_ref[:, span(h)]) for p, r, h in zip(dps, rqs, heads)]
        for i, (s, h) in enumerate(zip(slots, heads)):
            unit = q_ref[:, span(h)].astype(f32) * rqs[i]
            grad = rqs[i] * (dqs[i] - unit * jnp.sum(unit * dqs[i], axis=1, keepdims=True))
            gq_ref[:, span(h)] = grad.astype(bf16)
            dpq_s[s] = turned[i]
            f_t[s] = fts[i]
            s_t[s] = sts[i]

    def both(body, js, ours, theirs):
        slots = list(js) + [half + j for j in js]
        heads = [own_head(j) for j in js] + [other_head(j) for j in js]
        return body(slots, heads, [ours[j] for j in js] + [theirs[j] for j in js])

    for r in range(2):
        js = range(r * half // 2, (r + 1) * half // 2)
        enter(js)
        for j in js:
            wait_in(4, j, s_sib.at[j])
        made = both(forward, js, s_own, s_sib)
        for i, j in enumerate(js):
            c_both[core, j] = made[i]
            c_out[j] = made[len(js) + i]
        for j in js:
            push(5, j, c_out.at[j], c_both.at[core, j], sibling).start()
        if r == 0:
            both(query_grads, js, s_own, s_sib)
        join_grads(js)
    both(query_grads, js, s_own, s_sib)

    def drain_early(j, carry):
        push(0, j, out_map.at[j], out_map.at[j], sibling).wait_send()
        push(4, j, s_out.at[j], s_out.at[j], sibling).wait_send()
        push(5, j, c_out.at[j], c_out.at[j], sibling).wait_send()

        @pl.when(owner(j) != me)
        def _():
            push(1, j, chip_map.at[j], chip_map.at[j], sibling).wait_send()

        @pl.when(source(j) != me)
        def _():
            push(3, j, state_out.at[j], state_out.at[j], sibling).wait_send()

        return carry

    @pl.when(core == 0)
    def _():
        push(2, 0, state_out.at[half], state_out.at[half], sibling).wait_send()

    grad_out[half] = zero

    @pl.when(core == 1)
    def _():
        turned_grad = None
        for r in range(2):
            here = [half - 1 - i for i in range(r * half // 2, (r + 1) * half // 2)]
            for i in here:
                routed(6, i, c_got.at[i], source(i))
            for i in here:
                if turned_grad is None:
                    turned_grad = c_got[i].T
                else:
                    turned_grad = mm3(turned_grad, got_map[i][:, :BLOCK]) + c_got[i].T
                grad_out[i] = turned_grad.T
            for i in here:
                route(8, i, slot, grad_out.at[i + 1], grad_in.at[slot], source(i))
        push(7, 0, grad_out.at[0], gh_in.at[0], sibling).start()

    @pl.when(core == 0)
    def _():
        def lap(n, carry):
            i = half - 1 - n
            routed(6, i, c_got.at[i], source(i))
            grad_out[i] = mm3(map_t[i], grad_out[i + 1]) + c_got[i]
            return carry

        lax.fori_loop(0, half, lap, 0)
        wait_in(7, 0, gh_in.at[0])
        entry = gh_in[0]

        def lift(r, carry):
            for u in range(group):
                i = half - 1 - (r * group + u)
                grad_out[i + 1] = mm3(suffix[i + 1], entry) + grad_out[i + 1]
            for u in range(group):
                i = half - 1 - (r * group + u)
                route(8, i, slot, grad_out.at[i + 1], grad_in.at[slot], source(i))
            return carry

        lax.fori_loop(0, rounds, lift, 0)

    lax.fori_loop(0, half, drain_early, 0)

    def leave(js):
        for j in js:
            routed(8, j, grad_in.at[j], owner(j))
        lasts = [grad_in[j] for j in js]
        inners = [mm3(late_t[j], g) + c_both[1, j] for j, g in zip(js, lasts)]
        for j, a, b in zip(js, lasts, inners):
            g_own[j] = jnp.where(core == 0, b, a)
            g_out[j] = jnp.where(core == 0, a, b)
        for j in js:
            push(9, j, g_out.at[j], g_sib.at[j], sibling).start()

    def gate_terms(slots, heads, grads):
        row, col = masks()
        es = [e_s[s] + mm3(z_s[s], g) for s, g in zip(slots, grads)]
        efs = [jnp.where(row > col, mm3(e, f_t[s]), 0.0) for e, s in zip(es, slots)]
        ess = [mm3(e, s_t[s]) for e, s in zip(es, slots)]
        added = 0.0
        lane = lax.broadcasted_iota(jnp.int32, (BLOCK, BLOCK), 1)
        for i, (s, h) in enumerate(zip(slots, heads)):
            be = be_col[s]
            unit = k_ref[:, span(h)].astype(f32) * rk_col[s]
            gv_ref[:, span(h)] = (es[i] * be).astype(bf16)
            terms = es[i] * v_ref[:, span(h)].astype(f32) - ess[i] * unit - efs[i] * gram_s[s]
            dl = jnp.sum(terms, axis=1, keepdims=True) * (be * (1.0 - 2.0 * be))
            added = added + jnp.where(lane == s, dl, 0.0)
            p_s[s] = efs[i]
            p_t[s] = ess[i]
        dl_s[...] += added

    def key_grads(slots, heads, grads):
        gts = [g.T for g in grads]
        bes = [be_col[s] for s in slots]
        dks = [dpq_s[s] + mm3(f_s[s], gt) for s, gt in zip(slots, gts)]
        links = [p_s[s] * be for s, be in zip(slots, bes)]
        links = [(m + m.T) * rk_row[s] for m, s in zip(links, slots)]
        dks = [d - p_t[s] * be for d, s, be in zip(dks, slots, bes)]
        dks = [d - right_exact(m, k_ref[:, span(h)]) for d, m, h in zip(dks, links, heads)]
        for i, (s, h) in enumerate(zip(slots, heads)):
            rk = rk_col[s]
            unit = k_ref[:, span(h)].astype(f32) * rk
            grad = rk * (dks[i] - unit * jnp.sum(unit * dks[i], axis=1, keepdims=True))
            gk_ref[:, span(h)] = grad.astype(bf16)

    side = 2 ** (chips.bit_length() // 2)
    column, line = lax.div(chip, side), lax.rem(chip, side)
    start = column * (2 * side)
    at_row = 2 * line + core
    in_row = (2 * side, at_row, lambda i: {"seq": start + i})
    in_column = (chips // side, column, lambda i: {"seq": (i * side + line) * 2 + core})
    in_depth = (depth, layer, lambda i: {"dp": i})

    def swap(kind, ring, src, dst):
        count, here, target = ring
        made = []
        for d in range(1, count):
            i = lax.rem(here + d, count)
            copy = pltpu.make_async_remote_copy(
                src_ref=src(i), dst_ref=dst.at[here], send_sem=gate_send.at[kind, i],
                recv_sem=gate_recv.at[kind, here], device_id=target(i), device_id_type=MESH,
            )
            copy.start()
            made.append(copy)
        return made

    def summed(kind, ring, dst):
        arrive(kind, ring, dst)
        total = dst[0]
        for i in range(1, ring[0]):
            total = total + dst[i]
        return total

    def arrive(kind, ring, dst):
        count, here, target = ring
        for d in range(1, count):
            i = lax.rem(here + d, count)
            pltpu.make_async_remote_copy(
                src_ref=dst.at[i], dst_ref=dst.at[i], send_sem=gate_send.at[kind, i],
                recv_sem=gate_recv.at[kind, i], device_id=target(i), device_id_type=MESH,
            ).wait_recv()

    for r in range(2):
        js = range(r * half // 2, (r + 1) * half // 2)
        leave(js)
        for j in js:
            wait_in(9, j, g_sib.at[j])
        both(gate_terms, js, g_own, g_sib)

    rows = dl_s[...].T[: 2 * half]
    parts = jnp.concatenate([rows, rows - rows.astype(bf16).astype(f32)], axis=0).astype(bf16)
    product = mm(parts, x_ref[...])
    product = product[: 2 * half] + product[2 * half :]
    width = gate_out.shape[-1]
    for y in range(side):
        gate_out[2 * y + core] = product[:half, y * width : (y + 1) * width]
        gate_out[2 * y + 1 - core] = product[half:, y * width : (y + 1) * width]
    gate_in[at_row] = gate_out[at_row]
    copies = swap(0, in_row, lambda i: gate_out.at[i], gate_in)
    both(key_grads, range(half // 2), g_own, g_sib)
    total = summed(0, in_row, gate_in)
    column_out[0] = total
    column_in[column] = total
    copies += swap(1, in_column, lambda i: column_out.at[0], column_in)
    both(key_grads, range(half // 2, half), g_own, g_sib)
    total = summed(1, in_column, column_in)
    depth_out[0] = total
    depth_in[layer] = total
    copies += swap(2, in_depth, lambda i: depth_out.at[0], depth_in)

    def drain_late(j, carry):
        push(9, j, g_out.at[j], g_out.at[j], sibling).wait_send()

        @pl.when(owner(j) != me)
        def _():
            push(6, j, c_chip.at[j], c_chip.at[j], sibling).wait_send()

        @pl.when(source(j) != me)
        def _():
            push(8, j, grad_out.at[j + 1], grad_out.at[j + 1], sibling).wait_send()

        return carry

    lax.fori_loop(0, half, drain_late, 0)

    @pl.when(core == 1)
    def _():
        push(7, 0, grad_out.at[0], grad_out.at[0], sibling).wait_send()

    total = summed(2, in_depth, depth_in) * scale
    tile_out[0] = total
    tiles[at_row] = total
    last = swap(3, in_row, lambda i: tile_out.at[0], tiles)
    for copy in copies:
        copy.wait_send()
    arrive(3, in_row, tiles)
    for t in range(2 * side):
        tile = tiles[t]
        for r in range(half):
            at = 2 * r + t % 2
            gw_ref[at : at + 1, (t // 2) * width : (t // 2 + 1) * width] = tile[r : r + 1]
    for copy in last:
        copy.wait_send()


def publish(*refs):
    copies = [pltpu.make_async_copy(refs[i], refs[5 + i], refs[10].at[i]) for i in range(5)]
    for copy in copies:
        copy.start()
    for copy in copies:
        copy.wait()


def shards(chips, depth, queries, keys_in, values_in, inputs, target, gate_weight, beta_bias):
    heads = gate_weight.shape[1]
    width = heads * BLOCK
    half = heads // 2
    square = (BLOCK, BLOCK)

    def many(count, *tail, kind=f32):
        return pltpu.VMEM((count,) + (tail or square), kind)

    wide = (BLOCK, 2 * BLOCK)
    side = 2 ** (chips.bit_length() // 2)
    cut = inputs.shape[-1] // side
    scratch = [
        pltpu.VMEM((BLOCK, heads), f32), many(heads, BLOCK, 1), many(heads, BLOCK, 1), many(heads, BLOCK, 1),
        many(heads, 1, BLOCK),
        many(heads, kind=bf16), many(heads, kind=bf16),
    ] + [many(heads)] * 8 + [many(half)] * 2 + [many(heads)] * 6 + [
        pltpu.VMEM(square, f32),
        pltpu.VMEM((2, half) + wide, f32), many(half, *wide), many(half, *wide), many(half, *wide),
        many(half + 1, *wide), many(half + 1), many(1), many(half), many(half), many(half), many(half),
        pltpu.VMEM((2, half) + square, f32), many(half), many(half), many(half), many(half + 1), many(half),
        many(half + 1), many(1), many(half), many(half), many(half), many(half),
        many(2 * side, half, cut), many(2 * side, half, cut), many(1, half, cut), many(chips // side, half, cut),
        many(1, half, cut), many(depth, half, cut), many(1, half, cut), many(2 * side, half, cut),
        pltpu.SemaphoreType.DMA((10, half)), pltpu.SemaphoreType.DMA((10, half)),
        pltpu.SemaphoreType.DMA((4, 16)), pltpu.SemaphoreType.DMA((4, 16)),
    ]
    rows = jax.ShapeDtypeStruct((BLOCK, width), bf16)
    whole = pl.BlockSpec(memory_space=pltpu.VMEM)
    results = pl.pallas_call(
        functools.partial(kernel, chips, depth, 1.0 / math.sqrt(BLOCK * 2 * chips * depth)),
        out_shape=(rows, rows, rows, rows, jax.ShapeDtypeStruct((heads, inputs.shape[-1]), f32)),
        in_specs=[whole] * 7,
        out_specs=(whole,) * 5,
        scratch_shapes=scratch,
        compiler_params=pltpu.CompilerParams(
            collective_id=0, has_side_effects=True, vmem_limit_bytes=49 * 1024 * 1024
        ),
    )(queries[0], keys_in[0], values_in[0], inputs[0], target[0], gate_weight.T, beta_bias[None])
    anywhere = pl.BlockSpec(memory_space=pl.ANY)
    output, grad_q, grad_k, grad_v, grad_w = pl.pallas_call(
        publish,
        out_shape=tuple(jax.ShapeDtypeStruct(r.shape, r.dtype) for r in results),
        in_specs=[anywhere] * 5,
        out_specs=(anywhere,) * 5,
        scratch_shapes=[pltpu.SemaphoreType.DMA((5,))],
        compiler_params=pltpu.CompilerParams(vmem_limit_bytes=1024 * 1024),
    )(*results)
    return (output[None], grad_q[None], grad_k[None], grad_v[None], grad_w.T)


def solution(mesh):
    placed = P("dp", "seq", None)
    chips = mesh.shape["seq"] // 2
    return jax.shard_map(
        functools.partial(shards, chips, mesh.shape["dp"]),
        mesh=mesh,
        in_specs=(placed,) * 5 + (P(), P()),
        out_specs=(placed,) * 4 + (P(),),
        check_vma=False,
    )
```

```python
import functools
import math

import jax
import jax.numpy as jnp
from jax import lax
from jax.experimental import pallas as pl
from jax.experimental.pallas import tpu as pltpu
from jax.sharding import PartitionSpec as P

BLOCK = 128
EPSILON = 1e-06
GROUP = 8
f32 = jnp.float32
bf16 = jnp.bfloat16
MESH = pl.DeviceIdType.MESH


def mm(a, b):
    return jnp.dot(a, b, preferred_element_type=f32)


def mm_rows(a, b):
    return lax.dot_general(a, b, (((1,), (1,)), ((), ())), preferred_element_type=f32)


def mm3(a, b):
    return jnp.dot(a, b, preferred_element_type=f32, precision=lax.Precision.HIGH)


def mm3_rows(a, b):
    return lax.dot_general(a, b, (((1,), (1,)), ((), ())), preferred_element_type=f32, precision=lax.Precision.HIGH)


def split(x):
    high = x.astype(bf16)
    return high, (x - high.astype(f32)).astype(bf16)


def left_exact(exact, x):
    high, low = split(x)
    return mm(exact, high) + mm(exact, low)


def right_exact(x, exact):
    high, low = split(x)
    return mm(high, exact) + mm(low, exact)


def masks():
    row = lax.broadcasted_iota(jnp.int32, (BLOCK, BLOCK), 0)
    col = lax.broadcasted_iota(jnp.int32, (BLOCK, BLOCK), 1)
    return row, col


def unit_lower_inverse(systems):
    row, col = masks()
    apart = row ^ col
    eye = (row == col).astype(f32)
    inverses = [eye - jnp.where(apart < 2, a, 0.0) for a in systems]
    size = 2
    while size < BLOCK:
        band = (apart >= size) & (apart < 2 * size)
        packed = [x.astype(bf16) for x in inverses]
        steps = [mm(jnp.where(band, a, 0.0).astype(bf16), x) for a, x in zip(systems, packed)]
        steps = [mm(x, y.astype(bf16)) for x, y in zip(packed, steps)]
        inverses = [x - y for x, y in zip(inverses, steps)]
        size *= 2
    rest = [mm3(a, x) for a, x in zip(systems, inverses)]
    rest = [(eye - x - y) for x, y in zip(inverses, rest)]
    fixes = [mm(x.astype(bf16), y.astype(bf16)) for x, y in zip(inverses, rest)]
    return [x + y for x, y in zip(inverses, fixes)]


def kernel(
    chips, depth, scale,
    q_ref, k_ref, v_ref, x_ref, t_ref, w_ref, b_ref,
    o_ref, gq_ref, gk_ref, gv_ref, gw_ref,
    strength, rk_col, rq_col, be_col, rk_row,
    key_t, query_t, gram_s, inv_s, inv_t, wk_s, wv_s, p_s, p_t, z_s,
    early_t, late_t, f_s, f_t, s_t, do_s, e_s, dpq_s, dl_s,
    maps, out_map, chip_map, got_map, prefix, state_out, hand_in, state_in, s_own, s_sib, s_out,
    c_both, c_out, c_chip, c_got, suffix, map_t, grad_out, gh_in, grad_in, g_own, g_sib, g_out,
    gate_out, gate_in, column_out, column_in, depth_out, depth_in, tile_out, tiles,
    send, recv, gate_send, gate_recv,
):
    me = lax.axis_index("seq")
    core = lax.rem(me, 2)
    chip = lax.div(me, 2)
    half = chips // 2
    part = lax.div(chip, half)
    place = lax.rem(chip, half)
    across, along = lax.div(chip, 4), lax.rem(chip, 4)
    spread = chips == 16
    mine = 8 * lax.rem(across + along, 2) + 2 * across + lax.div(along, 2) if spread else chip
    parity = lax.rem(mine, 2)
    sibling = me + 1 - 2 * core
    rounds = half // min(GROUP, half)
    group = min(GROUP, half)

    def owner(j):
        head = 2 * j + core
        if spread:
            bank, seat = lax.div(head, 8), lax.rem(head, 8)
            line = lax.div(seat, 2)
            head = 4 * line + 2 * lax.rem(seat, 2) + lax.rem(line + bank, 2)
        return 2 * head + part

    def source(i):
        return 2 * (half * core + i) + parity

    def push(kind, at, src, dst, target):
        return pltpu.make_async_remote_copy(
            src_ref=src, dst_ref=dst, send_sem=send.at[kind, at], recv_sem=recv.at[kind, at],
            device_id={"seq": target}, device_id_type=MESH,
        )

    def wait_in(kind, at, dst):
        push(kind, at, dst, dst, sibling).wait_recv()

    def route(kind, send_at, recv_at, src, dst, target):
        @pl.when(target != me)
        def _():
            pltpu.make_async_remote_copy(
                src_ref=src, dst_ref=dst, send_sem=send.at[kind, send_at], recv_sem=recv.at[kind, recv_at],
                device_id={"seq": target}, device_id_type=MESH,
            ).start()

        @pl.when(target == me)
        def _():
            dst[...] = src[...]

    def routed(kind, at, dst, origin):
        @pl.when(origin != me)
        def _():
            wait_in(kind, at, dst)

    devices = 2 * chips
    layer = lax.axis_index("dp")

    def others(count, base, body, first=1):
        def run(d, carry):
            body(lax.rem(base + d, count))
            return carry

        lax.fori_loop(first, count, run, 0)

    barrier = pltpu.get_barrier_semaphore()
    others(devices, me, lambda t: pl.semaphore_signal(barrier, inc=1, device_id={"seq": t}, device_id_type=MESH))
    others(depth, layer, lambda t: pl.semaphore_signal(barrier, inc=1, device_id={"dp": t}, device_id_type=MESH))

    logits = mm_rows(x_ref[...], w_ref[...]) + b_ref[...]
    strength[...] = 0.5 / (1.0 + jnp.exp(-logits))
    dl_s[...] = jnp.zeros_like(dl_s)

    def span(head):
        return pl.ds(pl.multiple_of(head * BLOCK, BLOCK), BLOCK)

    def own_head(j):
        return 2 * j + core

    def other_head(j):
        return 2 * j + 1 - core

    def local_maps(slots, heads):
        row, col = masks()
        eye = row == col
        keys = [k_ref[:, span(h)] for h in heads]
        values = [v_ref[:, span(h)] for h in heads]
        strengths = strength[...]
        lane = lax.broadcasted_iota(jnp.int32, strengths.shape, 1)
        products = [mm_rows(key, key) for key in keys]
        norms = [jnp.where(eye, product, 0.0) for product in products]
        rks = [lax.rsqrt(jnp.sum(n, axis=1, keepdims=True) + EPSILON) for n in norms]
        rkr = [lax.rsqrt(jnp.sum(n, axis=0, keepdims=True) + EPSILON) for n in norms]
        bes = [jnp.sum(jnp.where(lane == h, strengths, 0.0), axis=1, keepdims=True) for h in heads]
        ber = [jnp.sum(jnp.where(eye, be, 0.0), axis=0, keepdims=True) for be in bes]
        grams = [jnp.where(row > col, m * a * b, 0.0) for m, a, b in zip(products, rks, rkr)]
        inverses = unit_lower_inverse([g * be for g, be in zip(grams, bes)])
        weights = [x * b for x, b in zip(inverses, ber)]
        wks = [right_exact(w * r, key) for w, r, key in zip(weights, rkr, keys)]
        wvs = [right_exact(w, value) for w, value in zip(weights, values)]
        keys_t = [key.T for key in keys]
        both = [
            left_exact(kt, jnp.concatenate([a, b], axis=1) * r) for kt, a, b, r in zip(keys_t, wks, wvs, rks)
        ]
        for i, s in enumerate(slots):
            rk_col[s] = rks[i]
            be_col[s] = bes[i]
            rk_row[s] = rkr[i]
            gram_s[s] = grams[i]
            inv_s[s] = inverses[i]
            wk_s[s] = wks[i]
            wv_s[s] = wvs[i]
            key_t[s] = keys_t[i]
        eyef = eye.astype(f32)
        return [jnp.concatenate([eyef - m[:, :BLOCK], m[:, BLOCK:]], axis=1) for m in both]

    def first(js):
        slots = [half + j for j in js] + list(js)
        heads = [other_head(j) for j in js] + [own_head(j) for j in js]
        made = local_maps(slots, heads)
        for i, j in enumerate(js):
            out_map[j] = made[i]
            maps[core, j] = made[len(js) + i]
        return slots, heads

    def compose_maps(js):
        for j in js:
            wait_in(0, j, maps.at[1 - core, j])
        nothing = jnp.zeros((BLOCK, BLOCK), f32)
        earlier = [maps[0, j] for j in js]
        later = [maps[1, j] for j in js]
        made = [mm3(b[:, :BLOCK], a) for a, b in zip(earlier, later)]
        for j, m, b in zip(js, made, later):
            chip_map[j] = m + jnp.concatenate([nothing, b[:, BLOCK:]], axis=1)
        for j in js:
            route(1, j, place, chip_map.at[j], got_map.at[place], owner(j))

    def score_terms(slots, heads):
        row, col = masks()
        keys = [k_ref[:, span(h)] for h in heads]
        queries = [q_ref[:, span(h)] for h in heads]
        rkr = [rk_row[s] for s in slots]
        products = [mm_rows(q, k) for q, k in zip(queries, keys)]
        wide = [q.astype(f32) for q in queries]
        rqs = [lax.rsqrt(jnp.sum(q * q, axis=1, keepdims=True) + EPSILON) for q in wide]
        ps = [jnp.where(row >= col, m * a * b, 0.0) for m, a, b in zip(products, rqs, rkr)]
        inverses_t = [inv_s[s].T for s in slots]
        zs = [right_exact(x * r, k) for x, r, k in zip(inverses_t, rkr, keys)]
        for i, s in enumerate(slots):
            rq_col[s] = rqs[i]
            p_s[s] = ps[i]
            p_t[s] = ps[i].T
            inv_t[s] = inverses_t[i]
            z_s[s] = zs[i]
            query_t[s] = queries[i].T

    for r in range(2):
        js = range(r * half // 2, (r + 1) * half // 2)
        slots, heads = first(js)
        if r == 0:
            pl.semaphore_wait(barrier, devices + depth - 2)
        for j in js:
            push(0, j, out_map.at[j], maps.at[core, j], sibling).start()
        score_terms(slots, heads)
        compose_maps(js)

    row, col = masks()
    eyef = (row == col).astype(f32)
    zero = jnp.zeros((BLOCK, BLOCK), f32)

    slot = lax.div(mine, 2)

    @pl.when(core == 0)
    def _():
        state_out[0] = zero
        turned_state = None
        for r in range(2):
            here = range(r * half // 2, (r + 1) * half // 2)
            for i in here:
                routed(1, i, got_map.at[i], source(i))
            for i in here:
                step = got_map[i]
                if turned_state is None:
                    turned_state = step[:, BLOCK:].T
                else:
                    turned_state = mm3_rows(turned_state, step[:, :BLOCK]) + step[:, BLOCK:].T
                state_out[i + 1] = turned_state.T
            for i in here:
                route(3, i, slot, state_out.at[i], state_in.at[slot], source(i))
        push(2, 0, state_out.at[half], hand_in.at[0], sibling).start()
        suffix[half] = eyef

        def back(n, carry):
            i = half - 1 - n
            turned = got_map[i][:, :BLOCK].T
            map_t[i] = turned
            suffix[i] = mm3(turned, suffix[i + 1])
            return carry

        lax.fori_loop(0, half, back, 0)

    @pl.when(core == 1)
    def _():
        prefix[0] = jnp.concatenate([eyef, zero], axis=1)

        def lap(i, carry):
            routed(1, i, got_map.at[i], source(i))
            step = got_map[i]
            map_t[i] = step[:, :BLOCK].T
            prefix[i + 1] = mm3(step[:, :BLOCK], prefix[i]) + jnp.concatenate([zero, step[:, BLOCK:]], axis=1)
            return carry

        lax.fori_loop(0, half, lap, 0)
        wait_in(2, 0, hand_in.at[0])
        entry = hand_in[0]

        def lift(r, carry):
            for u in range(group):
                i = r * group + u
                known = prefix[i]
                state_out[i] = mm3(known[:, :BLOCK], entry) + known[:, BLOCK:]
            for u in range(group):
                i = r * group + u
                route(3, i, slot, state_out.at[i], state_in.at[slot], source(i))
            return carry

        lax.fori_loop(0, rounds, lift, 0)

    for j in range(half):
        early_t[j] = maps[0, j][:, :BLOCK].T
        late_t[j] = maps[1, j][:, :BLOCK].T

    def enter(js):
        for j in js:
            routed(3, j, state_in.at[j], owner(j))
        firsts = [state_in[j] for j in js]
        steps_ = [maps[0, j] for j in js]
        seconds = [mm3(m[:, :BLOCK], a) + m[:, BLOCK:] for m, a in zip(steps_, firsts)]
        for j, a, b in zip(js, firsts, seconds):
            s_own[j] = jnp.where(core == 0, a, b)
            s_out[j] = jnp.where(core == 0, b, a)
        for j in js:
            push(4, j, s_out.at[j], s_sib.at[j], sibling).start()

    def forward(slots, heads, states):
        queries = [q_ref[:, span(h)] for h in heads]
        rqs = [rq_col[s] for s in slots]
        fresh = [wv_s[s] - mm3(wk_s[s], state) for s, state in zip(slots, states)]
        read = [left_exact(q, state) * r for q, state, r in zip(queries, states, rqs)]
        outs = [o + mm3(p_s[s], f) for o, f, s in zip(read, fresh, slots)]
        outs = [o.astype(bf16) for o in outs]
        cots = [o.astype(f32) - t_ref[:, span(h)].astype(f32) for o, h in zip(outs, heads)]
        ups = [mm3(p_t[s], d) for d, s in zip(cots, slots)]
        es = [mm3(inv_t[s], u) for u, s in zip(ups, slots)]
        cs = [left_exact(query_t[s], d * r) for s, d, r in zip(slots, cots, rqs)]
        cs = [c - left_exact(key_t[s], e * (rk_col[s] * be_col[s])) for c, s, e in zip(cs, slots, es)]
        for i, (s, h) in enumerate(zip(slots, heads)):
            o_ref[:, span(h)] = outs[i]
            f_s[s] = fresh[i]
            do_s[s] = cots[i]
            e_s[s] = es[i]
        return cs

    def join_grads(js):
        for j in js:
            wait_in(5, j, c_both.at[1 - core, j])
        made = [mm3(early_t[j], c_both[1, j]) + c_both[0, j] for j in js]
        for j, c in zip(js, made):
            c_chip[j] = c
        for j in js:
            route(6, j, place, c_chip.at[j], c_got.at[place], owner(j))

    def query_grads(slots, heads, states):
        row, col = masks()
        fts = [f_s[s].T for s in slots]
        sts = [state.T for state in states]
        cots = [do_s[s] for s in slots]
        rqs = [rq_col[s] for s in slots]
        dps = [jnp.where(row >= col, mm3(d, ft), 0.0) for d, ft in zip(cots, fts)]
        dqs = [mm3(d, st) for d, st in zip(cots, sts)]
        dqs = [
            d + right_exact(p * rk_row[s], k_ref[:, span(h)]) for d, p, s, h in zip(dqs, dps, slots, heads)
        ]
        turned = [right_exact((p * r).T, q_ref[:, span(h)]) for p, r, h in zip(dps, rqs, heads)]
        for i, (s, h) in enumerate(zip(slots, heads)):
            unit = q_ref[:, span(h)].astype(f32) * rqs[i]
            grad = rqs[i] * (dqs[i] - unit * jnp.sum(unit * dqs[i], axis=1, keepdims=True))
            gq_ref[:, span(h)] = grad.astype(bf16)
            dpq_s[s] = turned[i]
            f_t[s] = fts[i]
            s_t[s] = sts[i]

    def both(body, js, ours, theirs):
        slots = list(js) + [half + j for j in js]
        heads = [own_head(j) for j in js] + [other_head(j) for j in js]
        return body(slots, heads, [ours[j] for j in js] + [theirs[j] for j in js])

    for r in range(2):
        js = range(r * half // 2, (r + 1) * half // 2)
        enter(js)
        for j in js:
            wait_in(4, j, s_sib.at[j])
        made = both(forward, js, s_own, s_sib)
        for i, j in enumerate(js):
            c_both[core, j] = made[i]
            c_out[j] = made[len(js) + i]
        for j in js:
            push(5, j, c_out.at[j], c_both.at[core, j], sibling).start()
        if r == 0:
            both(query_grads, js, s_own, s_sib)
        join_grads(js)
    both(query_grads, js, s_own, s_sib)

    def drain_early(j, carry):
        push(0, j, out_map.at[j], out_map.at[j], sibling).wait_send()
        push(4, j, s_out.at[j], s_out.at[j], sibling).wait_send()
        push(5, j, c_out.at[j], c_out.at[j], sibling).wait_send()

        @pl.when(owner(j) != me)
        def _():
            push(1, j, chip_map.at[j], chip_map.at[j], sibling).wait_send()

        @pl.when(source(j) != me)
        def _():
            push(3, j, state_out.at[j], state_out.at[j], sibling).wait_send()

        return carry

    @pl.when(core == 0)
    def _():
        push(2, 0, state_out.at[half], state_out.at[half], sibling).wait_send()

    grad_out[half] = zero

    @pl.when(core == 1)
    def _():
        turned_grad = None
        for r in range(2):
            here = [half - 1 - i for i in range(r * half // 2, (r + 1) * half // 2)]
            for i in here:
                routed(6, i, c_got.at[i], source(i))
            for i in here:
                if turned_grad is None:
                    turned_grad = c_got[i].T
                else:
                    turned_grad = mm3(turned_grad, got_map[i][:, :BLOCK]) + c_got[i].T
                grad_out[i] = turned_grad.T
            for i in here:
                route(8, i, slot, grad_out.at[i + 1], grad_in.at[slot], source(i))
        push(7, 0, grad_out.at[0], gh_in.at[0], sibling).start()

    @pl.when(core == 0)
    def _():
        def lap(n, carry):
            i = half - 1 - n
            routed(6, i, c_got.at[i], source(i))
            grad_out[i] = mm3(map_t[i], grad_out[i + 1]) + c_got[i]
            return carry

        lax.fori_loop(0, half, lap, 0)
        wait_in(7, 0, gh_in.at[0])
        entry = gh_in[0]

        def lift(r, carry):
            for u in range(group):
                i = half - 1 - (r * group + u)
                grad_out[i + 1] = mm3(suffix[i + 1], entry) + grad_out[i + 1]
            for u in range(group):
                i = half - 1 - (r * group + u)
                route(8, i, slot, grad_out.at[i + 1], grad_in.at[slot], source(i))
            return carry

        lax.fori_loop(0, rounds, lift, 0)

    lax.fori_loop(0, half, drain_early, 0)

    def leave(js):
        for j in js:
            routed(8, j, grad_in.at[j], owner(j))
        lasts = [grad_in[j] for j in js]
        inners = [mm3(late_t[j], g) + c_both[1, j] for j, g in zip(js, lasts)]
        for j, a, b in zip(js, lasts, inners):
            g_own[j] = jnp.where(core == 0, b, a)
            g_out[j] = jnp.where(core == 0, a, b)
        for j in js:
            push(9, j, g_out.at[j], g_sib.at[j], sibling).start()

    def gate_terms(slots, heads, grads):
        row, col = masks()
        es = [e_s[s] + mm3(z_s[s], g) for s, g in zip(slots, grads)]
        efs = [jnp.where(row > col, mm3(e, f_t[s]), 0.0) for e, s in zip(es, slots)]
        ess = [mm3(e, s_t[s]) for e, s in zip(es, slots)]
        added = 0.0
        lane = lax.broadcasted_iota(jnp.int32, (BLOCK, BLOCK), 1)
        for i, (s, h) in enumerate(zip(slots, heads)):
            be = be_col[s]
            unit = k_ref[:, span(h)].astype(f32) * rk_col[s]
            gv_ref[:, span(h)] = (es[i] * be).astype(bf16)
            terms = es[i] * v_ref[:, span(h)].astype(f32) - ess[i] * unit - efs[i] * gram_s[s]
            dl = jnp.sum(terms, axis=1, keepdims=True) * (be * (1.0 - 2.0 * be))
            added = added + jnp.where(lane == s, dl, 0.0)
            p_s[s] = efs[i]
            p_t[s] = ess[i]
        dl_s[...] += added

    def key_grads(slots, heads, grads):
        gts = [g.T for g in grads]
        bes = [be_col[s] for s in slots]
        dks = [dpq_s[s] + mm3(f_s[s], gt) for s, gt in zip(slots, gts)]
        links = [p_s[s] * be for s, be in zip(slots, bes)]
        links = [(m + m.T) * rk_row[s] for m, s in zip(links, slots)]
        dks = [d - p_t[s] * be for d, s, be in zip(dks, slots, bes)]
        dks = [d - right_exact(m, k_ref[:, span(h)]) for d, m, h in zip(dks, links, heads)]
        for i, (s, h) in enumerate(zip(slots, heads)):
            rk = rk_col[s]
            unit = k_ref[:, span(h)].astype(f32) * rk
            grad = rk * (dks[i] - unit * jnp.sum(unit * dks[i], axis=1, keepdims=True))
            gk_ref[:, span(h)] = grad.astype(bf16)

    side = 2 ** (chips.bit_length() // 2)
    column, line = lax.div(chip, side), lax.rem(chip, side)
    start = column * (2 * side)
    at_row = 2 * line + core
    in_row = (2 * side, at_row, lambda i: {"seq": start + i})
    in_column = (chips // side, column, lambda i: {"seq": (i * side + line) * 2 + core})
    in_depth = (depth, layer, lambda i: {"dp": i})

    def swap(kind, ring, src, dst):
        count, here, target = ring
        made = []
        for d in range(1, count):
            i = lax.rem(here + d, count)
            copy = pltpu.make_async_remote_copy(
                src_ref=src(i), dst_ref=dst.at[here], send_sem=gate_send.at[kind, i],
                recv_sem=gate_recv.at[kind, here], device_id=target(i), device_id_type=MESH,
            )
            copy.start()
            made.append(copy)
        return made

    def summed(kind, ring, dst):
        arrive(kind, ring, dst)
        total = dst[0]
        for i in range(1, ring[0]):
            total = total + dst[i]
        return total

    def arrive(kind, ring, dst):
        count, here, target = ring
        for d in range(1, count):
            i = lax.rem(here + d, count)
            pltpu.make_async_remote_copy(
                src_ref=dst.at[i], dst_ref=dst.at[i], send_sem=gate_send.at[kind, i],
                recv_sem=gate_recv.at[kind, i], device_id=target(i), device_id_type=MESH,
            ).wait_recv()

    for r in range(2):
        js = range(r * half // 2, (r + 1) * half // 2)
        leave(js)
        for j in js:
            wait_in(9, j, g_sib.at[j])
        both(gate_terms, js, g_own, g_sib)

    rows = dl_s[...].T[: 2 * half]
    parts = jnp.concatenate([rows, rows - rows.astype(bf16).astype(f32)], axis=0).astype(bf16)
    product = mm(parts, x_ref[...])
    product = product[: 2 * half] + product[2 * half :]
    width = gate_out.shape[-1]
    for y in range(side):
        gate_out[2 * y + core] = product[:half, y * width : (y + 1) * width]
        gate_out[2 * y + 1 - core] = product[half:, y * width : (y + 1) * width]
    gate_in[at_row] = gate_out[at_row]
    copies = swap(0, in_row, lambda i: gate_out.at[i], gate_in)
    both(key_grads, range(half // 2), g_own, g_sib)
    total = summed(0, in_row, gate_in)
    column_out[0] = total
    column_in[column] = total
    copies += swap(1, in_column, lambda i: column_out.at[0], column_in)
    both(key_grads, range(half // 2, half), g_own, g_sib)
    total = summed(1, in_column, column_in)
    depth_out[0] = total
    depth_in[layer] = total
    copies += swap(2, in_depth, lambda i: depth_out.at[0], depth_in)

    def drain_late(j, carry):
        push(9, j, g_out.at[j], g_out.at[j], sibling).wait_send()

        @pl.when(owner(j) != me)
        def _():
            push(6, j, c_chip.at[j], c_chip.at[j], sibling).wait_send()

        @pl.when(source(j) != me)
        def _():
            push(8, j, grad_out.at[j + 1], grad_out.at[j + 1], sibling).wait_send()

        return carry

    lax.fori_loop(0, half, drain_late, 0)

    @pl.when(core == 1)
    def _():
        push(7, 0, grad_out.at[0], grad_out.at[0], sibling).wait_send()

    total = summed(2, in_depth, depth_in) * scale
    tile_out[0] = total
    tiles[at_row] = total
    last = swap(3, in_row, lambda i: tile_out.at[0], tiles)
    for copy in copies:
        copy.wait_send()
    arrive(3, in_row, tiles)
    for t in range(2 * side):
        tile = tiles[t]
        for r in range(half):
            at = 2 * r + t % 2
            gw_ref[at : at + 1, (t // 2) * width : (t // 2 + 1) * width] = tile[r : r + 1]
    for copy in last:
        copy.wait_send()


def publish(*refs):
    copies = [pltpu.make_async_copy(refs[i], refs[5 + i], refs[10].at[i]) for i in range(5)]
    for copy in copies:
        copy.start()
    for copy in copies:
        copy.wait()


def shards(chips, depth, queries, keys_in, values_in, inputs, target, gate_weight, beta_bias):
    heads = gate_weight.shape[1]
    width = heads * BLOCK
    half = heads // 2
    square = (BLOCK, BLOCK)

    def many(count, *tail, kind=f32):
        return pltpu.VMEM((count,) + (tail or square), kind)

    wide = (BLOCK, 2 * BLOCK)
    side = 2 ** (chips.bit_length() // 2)
    cut = inputs.shape[-1] // side
    scratch = [
        pltpu.VMEM((BLOCK, heads), f32), many(heads, BLOCK, 1), many(heads, BLOCK, 1), many(heads, BLOCK, 1),
        many(heads, 1, BLOCK),
        many(heads, kind=bf16), many(heads, kind=bf16),
    ] + [many(heads)] * 8 + [many(half)] * 2 + [many(heads)] * 6 + [
        pltpu.VMEM(square, f32),
        pltpu.VMEM((2, half) + wide, f32), many(half, *wide), many(half, *wide), many(half, *wide),
        many(half + 1, *wide), many(half + 1), many(1), many(half), many(half), many(half), many(half),
        pltpu.VMEM((2, half) + square, f32), many(half), many(half), many(half), many(half + 1), many(half),
        many(half + 1), many(1), many(half), many(half), many(half), many(half),
        many(2 * side, half, cut), many(2 * side, half, cut), many(1, half, cut), many(chips // side, half, cut),
        many(1, half, cut), many(depth, half, cut), many(1, half, cut), many(2 * side, half, cut),
        pltpu.SemaphoreType.DMA((10, half)), pltpu.SemaphoreType.DMA((10, half)),
        pltpu.SemaphoreType.DMA((4, 16)), pltpu.SemaphoreType.DMA((4, 16)),
    ]
    rows = jax.ShapeDtypeStruct((BLOCK, width), bf16)
    whole = pl.BlockSpec(memory_space=pltpu.VMEM)
    results = pl.pallas_call(
        functools.partial(kernel, chips, depth, 1.0 / math.sqrt(BLOCK * 2 * chips * depth)),
        out_shape=(rows, rows, rows, rows, jax.ShapeDtypeStruct((heads, inputs.shape[-1]), f32)),
        in_specs=[whole] * 7,
        out_specs=(whole,) * 5,
        scratch_shapes=scratch,
        compiler_params=pltpu.CompilerParams(
            collective_id=0, has_side_effects=True, vmem_limit_bytes=51 * 1024 * 1024
        ),
    )(queries[0], keys_in[0], values_in[0], inputs[0], target[0], gate_weight.T, beta_bias[None])
    anywhere = pl.BlockSpec(memory_space=pl.ANY)
    output, grad_q, grad_k, grad_v, grad_w = pl.pallas_call(
        publish,
        out_shape=tuple(jax.ShapeDtypeStruct(r.shape, r.dtype) for r in results),
        in_specs=[anywhere] * 5,
        out_specs=(anywhere,) * 5,
        scratch_shapes=[pltpu.SemaphoreType.DMA((5,))],
        compiler_params=pltpu.CompilerParams(vmem_limit_bytes=1024 * 1024),
    )(*results)
    return (output[None], grad_q[None], grad_k[None], grad_v[None], grad_w.T)


def solution(mesh):
    placed = P("dp", "seq", None)
    chips = mesh.shape["seq"] // 2
    return jax.shard_map(
        functools.partial(shards, chips, mesh.shape["dp"]),
        mesh=mesh,
        in_specs=(placed,) * 5 + (P(), P()),
        out_specs=(placed,) * 4 + (P(),),
        check_vma=False,
    )
```
